128 devices in a mesh: dp: 4 (over z), ep: 32 (over x, y, core).
Axes of the slice: x: 4, y: 4, z: 4, core: 2. Of those that a mesh axis runs over, the one named last changes fastest.
Arguments:
- hidden_in: bfloat16 [2, 2048, 8, 1024], P(None, ('dp', 'ep')), parts along dimension 1, may hold values from -6 to 6
- expert_ids: int32 [2, 2048, 8], P(None, ('dp', 'ep')), parts along dimension 1, may hold values from 0 to 63, as said below
- gates: float32 [2, 2048, 8], P(None, ('dp', 'ep')), parts along dimension 1, may hold values from 0.1 to 1
- expert_weight: bfloat16 [64, 1024, 3584], P('ep'), may hold values from -0.1875 to 0.1875
- column_scale: bfloat16 [64, 3584], P('ep'), may hold values from 0.5 to 2
- replica_map: int32 [128], P('dp'), parts along dimension 0, may hold values from 0 to 63, as said below
Outputs:
- combined: bfloat16 [2, 2048, 3584], P(None, ('dp', 'ep')), parts along dimension 1
- replica_weight: bfloat16 [128, 1024, 3584], P(('dp', 'ep')), parts along dimension 0
- replica_scale: bfloat16 [128, 3584], P(('dp', 'ep')), parts along dimension 0
The draws below stay inside these ranges and needn't reach their ends.
There are 4 independent parts, one for each index of `dp`. The reference program is written for one: setup_inputs(seed, part) draws one part's arguments, and reference() takes and returns one part's arrays. A program takes and returns all parts, laid end to end along the dimension named above; an argument that names none is the same for every part. Nothing has to cross between parts.
Inputs may be any that keep to these rules, and one draw needn't show every extreme that they name: `expert_ids`: each token names 8 different experts. Within one step, the 16 tokens of one device name exactly one expert 2 * 4 times, and that expert is listed in replica_map; they name every other expert at most 2 times. `replica_map`: entry d is one of the two experts owned by device (d + 16) mod 32, that is 2 * ((d + 16) mod 32) or one more; entries are distinct.
All inputs are finite; a program needn't handle non-finite values.
Results may differ from the reference program's by a relative error of at most 0.0049.
Values may be sent and summed in bfloat16 or wider, within the bound.
No kernel may reach another device: no remote copies, remote signals or barrier semaphores. Data moves between devices by JAX's collectives and lax.ppermute only.
A program may use at most 128 MiB of HBM per device.

```python
import math
import jax
import jax.numpy as jnp
from jax import lax

OUT_DIM = 3584
HIDDEN_SIZE = 1024
TOPK = 8
ROWS = 16
STEPS = 2
EXPERTS = 64
TOKENS = 512
CAP = 4
N_EP = 32


def replica_choice(key):
    host_index = jnp.arange(N_EP, dtype=jnp.int32)
    pick_bits = jax.random.randint(jax.random.fold_in(key, 11), (N_EP,), 0, 2, dtype=jnp.int32)
    return (2 * ((host_index + N_EP // 2) % N_EP) + pick_bits).astype(jnp.int32)


def draw_replica_map(key, part):
    return replica_choice(key)


def shuffle_experts(subkey):
    return jax.random.permutation(subkey, EXPERTS)


def draw_expert_ids(key, part):
    replica_list = replica_choice(key)
    block_total = STEPS * N_EP
    chooser = jax.random.randint(jax.random.fold_in(key, 12), (block_total,), 0, N_EP, dtype=jnp.int32)
    forced_expert = replica_list[chooser]
    shuffle_keys = jax.random.split(jax.random.fold_in(key, 13), block_total)
    shuffled = jax.vmap(shuffle_experts)(shuffle_keys).astype(jnp.int32)
    is_forced = (shuffled == forced_expert[:, None]).astype(jnp.int32)
    arranged = jnp.argsort(is_forced, axis=1, stable=True)
    cold_list = jnp.take_along_axis(shuffled, arranged, axis=1)[:, :EXPERTS - 1]
    forced_rows = 2 * CAP
    row_index = jnp.arange(ROWS, dtype=jnp.int32)[:, None]
    column_index = jnp.arange(TOPK, dtype=jnp.int32)[None, :]
    lead_rows = (row_index < forced_rows).astype(jnp.int32)
    start_at = (TOPK - 1) * jnp.minimum(row_index, forced_rows) + TOPK * jnp.maximum(row_index - forced_rows, 0)
    cold_at = (start_at + column_index - lead_rows + (EXPERTS - 1)) % (EXPERTS - 1)
    cold_pick = cold_list[:, cold_at]
    first_column = (column_index == 0) & (row_index < forced_rows)
    table = jnp.where(first_column[None], forced_expert[:, None, None], cold_pick)
    row_scores = jax.random.randint(jax.random.fold_in(key, 14), (block_total, ROWS), 0, 65536, dtype=jnp.int32)
    row_scores = row_scores * ROWS + jnp.arange(ROWS, dtype=jnp.int32)[None, :]
    row_order = jnp.argsort(row_scores, axis=1)
    table = jnp.take_along_axis(table, row_order[:, :, None], axis=1)
    column_scores = jax.random.randint(jax.random.fold_in(key, 15), (block_total, ROWS, TOPK), 0, 65536, dtype=jnp.int32)
    column_scores = column_scores * TOPK + jnp.arange(TOPK, dtype=jnp.int32)[None, None, :]
    column_order = jnp.argsort(column_scores, axis=2)
    table = jnp.take_along_axis(table, column_order, axis=2)
    return table.reshape(STEPS, N_EP * ROWS, TOPK).astype(jnp.int32)


def block_scale(rng, extent, cuts, least, largest):
    level = 1.0
    for axis_at, shards_of in cuts:
        draws = jax.random.uniform(jax.random.fold_in(jax.random.fold_in(rng, 6), axis_at), (shards_of,), jnp.float32, least / len(cuts), largest / len(cuts))
        level = level * jnp.repeat(jnp.exp(draws), extent[axis_at] // shards_of).reshape((-1,) + (1,) * (len(extent) - 1 - axis_at))
    return level


def bell_draw(own_key, shape, deviation, most, pieces=(), kind=jnp.bfloat16):
    result = deviation * jax.random.normal(own_key, shape, jnp.float32)
    if pieces:
        result = result * block_scale(own_key, shape, pieces, -0.22, 0.18)
    return jnp.clip(result, -most, most).astype(kind)


def setup_inputs(seed: int = 0, part: int = 0) -> dict:
    key_list = jax.random.split(jax.random.key(seed), 7)
    part_keys = jax.random.split(jax.random.fold_in(key_list[6], part), 7)
    return {
        "hidden_in": bell_draw(part_keys[0], (STEPS, TOKENS, TOPK, HIDDEN_SIZE), 1.0, 6.0, ((1, 32),)),
        "expert_ids": draw_expert_ids(jax.random.fold_in(jax.random.fold_in(key_list[6], part), 71), part),
        "gates": jnp.clip(jnp.exp(math.log(1.0) - 2.3025851 * jax.random.uniform(part_keys[2], (STEPS, TOKENS, TOPK), jnp.float32) ** block_scale(part_keys[2], (STEPS, TOKENS, TOPK), ((1, 32),), -0.2, 0.2)), 0.1, 1.0),
        "expert_weight": bell_draw(key_list[3], (EXPERTS, HIDDEN_SIZE, OUT_DIM), HIDDEN_SIZE ** -0.5, 0.1875, ((0, 32),)),
        "column_scale": jnp.clip(jnp.exp(math.log(2.0) - 1.3862944 * jax.random.uniform(key_list[4], (EXPERTS, OUT_DIM), jnp.float32) ** block_scale(key_list[4], (EXPERTS, OUT_DIM), ((0, 32),), -0.2, 0.2)), 0.5, 2.0).astype(jnp.bfloat16),
        "replica_map": draw_replica_map(jax.random.fold_in(jax.random.fold_in(key_list[6], part), 71), part),
    }


def reference(hidden_in, expert_ids, gates, expert_weight, column_scale, replica_map):
    replica_weight = jnp.take(expert_weight, replica_map, axis=0)
    replica_scale = jnp.take(column_scale, replica_map, axis=0)
    item_total = ROWS * N_EP * TOPK
    capacity_rows = min(item_total, 2 * CAP * N_EP)
    positions = jnp.arange(item_total, dtype=jnp.int32)
    results = []
    for step_index in range(STEPS):
        activations = hidden_in[step_index].reshape(item_total, HIDDEN_SIZE)
        expert_list = expert_ids[step_index].reshape(item_total).astype(jnp.int32)

        def expert_pass(collected, expert):
            sort_keys = jnp.where(expert_list == expert, 0, item_total).astype(jnp.int32) + positions
            chosen = jnp.argsort(sort_keys)[:capacity_rows].astype(jnp.int32)
            gathered = jnp.take(activations, chosen, axis=0)
            product = jnp.dot(gathered, expert_weight[expert], preferred_element_type=jnp.float32)
            product = (product * column_scale[expert].astype(jnp.float32)[None, :]).astype(jnp.bfloat16)
            matched = jnp.take(expert_list, chosen) == expert
            where_to = jnp.where(matched, chosen, item_total).astype(jnp.int32)
            collected = collected.at[where_to].set(product, mode="drop")
            return collected, None

        initial = jnp.zeros((item_total, OUT_DIM), jnp.bfloat16)
        expert_out, _ = lax.scan(expert_pass, initial, jnp.arange(EXPERTS, dtype=jnp.int32))
        weighted = expert_out.astype(jnp.float32).reshape(ROWS * N_EP, TOPK, OUT_DIM)
        weighted = weighted * gates[step_index].astype(jnp.float32)[:, :, None]
        results.append(jnp.sum(weighted, axis=1).astype(jnp.bfloat16))
    return jnp.stack(results, 0), replica_weight, replica_scale
```

```python
import jax
import jax.numpy as jnp
from jax import lax
from jax.sharding import Mesh, PartitionSpec as P

EP = ("x", "y", "c")
WEIGHT_ROWS = (64, 64, 64, 64)
HALVES = 2


def shifted(block, axis, distance):
    count = lax.axis_size(axis)
    return lax.ppermute(block, axis, [(i, (i + distance) % count) for i in range(count)])


def replica_update(expert_weight, column_scale, replica_map):
    part, parts = lax.axis_index("dp"), lax.axis_size("dp")
    me = lax.axis_index(EP)
    depth, width = expert_weight.shape[1:]
    quarter = depth // parts
    half_axis = lax.axis_size("x") // 2
    crossed, at = [], 0
    for rows in WEIGHT_ROWS:
        block = lax.dynamic_slice(expert_weight, (0, part * quarter + at, 0), (2, rows, width))
        crossed.append(shifted(block, "x", half_axis))
        at += rows
    partner = replica_map[(me + lax.axis_size(EP) // 2) % lax.axis_size(EP)]
    scale = lax.dynamic_index_in_dim(column_scale, partner - 2 * me, 0, keepdims=True)
    replica_scale = shifted(scale, "x", half_axis)
    picks = lax.all_gather(replica_map, "dp").reshape(parts, -1)[:, me] % 2
    pieces = []
    for block in crossed:
        chosen = jnp.where(picks[:, None, None] == 0, block[0][None], block[1][None])
        pieces.append(lax.all_to_all(chosen, "dp", 0, 0, tiled=True))
    return jnp.concatenate(pieces, 1).reshape(1, depth, width), replica_scale


def rank_of(expert_list):
    count = expert_list.shape[-1]
    order = jnp.arange(count, dtype=jnp.int32)
    same = expert_list[..., :, None] == expert_list[..., None, :]
    return jnp.sum(same & (order[:, None] > order[None, :]), axis=-1, dtype=jnp.int32)


def local(hidden_in, expert_ids, gates, expert_weight, column_scale, replica_map):
    steps, rows, top, depth = hidden_in.shape
    width = expert_weight.shape[2]
    items = rows * top
    n_x, n_yc, n_ep = lax.axis_size("x"), lax.axis_size("y") * lax.axis_size("c"), lax.axis_size(EP)
    my_x, my_yc, me = lax.axis_index("x"), lax.axis_index(("y", "c")), lax.axis_index(EP)

    replica_weight, replica_scale = replica_update(expert_weight, column_scale, replica_map)

    expert_list = expert_ids.reshape(steps, items)
    rank = rank_of(expert_list)
    step_of = jnp.arange(steps, dtype=jnp.int32)[:, None]
    place = jnp.where(
        rank < 2,
        (expert_list // 2) * 8 + (expert_list % 2) * 4 + step_of * 2 + rank,
        n_ep * 8 + step_of * 8 + rank - 2,
    ).reshape(steps * items)
    selector = (
        jnp.arange(n_ep * 8 + 16, dtype=jnp.int32)[:, None] == place[None, :]
    ).astype(jnp.bfloat16)
    outgoing = jnp.dot(
        selector, hidden_in.reshape(steps * items, depth), preferred_element_type=jnp.float32
    ).astype(jnp.bfloat16)
    hot_id = jnp.sum(jnp.where(rank == 7, expert_list, 0), axis=1)
    flat_gates = gates.reshape(steps * items)
    high = lax.reduce_precision(flat_gates, 8, 7)
    middle = lax.reduce_precision(flat_gates - high, 8, 7)
    low = flat_gates - high - middle
    told = jnp.concatenate(
        [expert_list.reshape(steps * items).astype(jnp.float32), high, middle, low]
    ).astype(jnp.bfloat16)
    line = jnp.arange(16, dtype=jnp.int32)[:, None]
    hot_line = jnp.where(line < 8, hot_id[0], hot_id[1]).astype(jnp.bfloat16)
    hot_block = jnp.where(line == 6, told[None, :], outgoing[n_ep * 8 :])
    hot_block = jnp.where(line % 8 == 7, hot_line, hot_block)
    received = lax.all_to_all(
        outgoing[: n_ep * 8].reshape(n_ep, 8, depth), EP, 0, 0, tiled=True
    )
    hot_all = lax.all_gather(hot_block, EP)

    normal = received.reshape(n_x, n_yc, 8, depth).transpose(1, 0, 2, 3).reshape(n_yc, n_x * 8, depth)
    normal_lane = jnp.broadcast_to((jnp.arange(n_x * 8, dtype=jnp.int32) % 8) // 4, (n_yc, n_x * 8))
    by_step = hot_all.reshape(n_x, n_yc, steps, 8, depth).transpose(1, 0, 2, 3, 4)
    hot = by_step[:, :, :, :6].reshape(n_yc, n_x * 12, depth)
    hot_lane = by_step[:, :, :, 7, 0].astype(jnp.int32) - 2 * me
    hot_lane = jnp.broadcast_to(hot_lane[..., None], (n_yc, n_x, steps, 6)).reshape(n_yc, n_x * 12)
    stack = n_x * 20
    served = jnp.concatenate([normal, hot], 1).reshape(n_yc * stack, depth)
    lane = jnp.concatenate([normal_lane, hot_lane], 1).reshape(n_yc * stack, 1)
    zero = jnp.zeros((), jnp.bfloat16)
    spread = jnp.concatenate(
        [jnp.where(lane == 0, served, zero), jnp.where(lane == 1, served, zero)], 1
    )

    told_all = hot_all.reshape(n_x, n_yc, 16, depth)[:, :, 6]
    told_here = lax.dynamic_index_in_dim(told_all, my_yc, 1, keepdims=False)
    told_here = told_here.astype(jnp.float32).reshape(n_x, 4, steps, items)
    ids_here = told_here[:, 0].astype(jnp.int32)
    gates_here = told_here[:, 1] + told_here[:, 2] + told_here[:, 3]
    rank_here = rank_of(ids_here)
    who = jnp.arange(n_x * steps, dtype=jnp.int32).reshape(n_x, steps, 1) * 256
    code = jnp.where(rank_here < 2, ids_here * 2 + rank_here, 128 + rank_here - 2) + who
    source = jnp.arange(n_yc, dtype=jnp.int32)[:, None]
    row = jnp.arange(n_x * 8, dtype=jnp.int32)[None, :]
    normal_code = ((n_yc * my_x + source) * 2 + (row % 8) // 4) * 2 + row % 2
    normal_code = normal_code + ((row // 8) * steps + (row % 4) // 2) * 256
    row = jnp.arange(n_x * 12, dtype=jnp.int32)[None, :]
    hot_code = 128 + row % 6 + ((row // 12) * steps + (row % 12) // 6) * 256
    hot_code = jnp.broadcast_to(hot_code, (n_yc, n_x * 12))
    column_code = jnp.concatenate([normal_code, hot_code], 1).reshape(n_yc * stack)
    code = code.reshape(n_x * steps * rows, top)
    gates_here = gates_here.reshape(n_x * steps * rows, top)
    mix = jnp.sum(
        jnp.where(code[:, :, None] == column_code[None, None, :], gates_here[:, :, None], 0.0), axis=1
    )
    mix_high = lax.reduce_precision(mix, 8, 7)
    mixes = jnp.concatenate([mix_high, mix - mix_high], 0).astype(jnp.bfloat16)

    flat_weight = expert_weight.reshape(2 * depth, width)
    scales = column_scale.astype(jnp.float32)
    piece = width // HALVES
    results = []
    for half in range(HALVES):
        columns = slice(half * piece, (half + 1) * piece)
        product = jnp.dot(spread, flat_weight[:, columns], preferred_element_type=jnp.float32)
        product = product * jnp.where(lane == 0, scales[0:1, columns], scales[1:2, columns])
        product = product.astype(jnp.bfloat16).reshape(n_yc, stack, piece)
        returned = lax.all_to_all(product, ("y", "c"), 0, 0, tiled=True)
        partial = jnp.dot(
            mixes, returned.reshape(n_yc * stack, piece), preferred_element_type=jnp.float32
        )
        many = n_x * steps * rows
        partial = (partial[:many] + partial[many:]).astype(jnp.bfloat16)
        partial = lax.all_to_all(partial.reshape(n_x, steps * rows, piece), "x", 0, 0, tiled=True)
        total = jnp.sum(partial.astype(jnp.float32), axis=0).astype(jnp.bfloat16)
        results.append(total.reshape(steps, rows, piece))
    return jnp.concatenate(results, 2), replica_weight, replica_scale


def solution(mesh):
    n_dp = mesh.shape["dp"]
    grid = Mesh(mesh.devices.reshape(n_dp, 4, 4, 2), ("dp", "x", "y", "c"))
    everywhere = ("dp",) + EP
    in_specs = (
        P(None, everywhere, None, None),
        P(None, everywhere, None),
        P(None, everywhere, None),
        P(EP, None, None),
        P(EP, None),
        P("dp"),
    )
    out_specs = (P(None, everywhere, None), P(everywhere, None, None), P(everywhere, None))
    return jax.shard_map(local, mesh=grid, in_specs=in_specs, out_specs=out_specs, check_vma=False)
```

```python
import functools

import jax
import jax.numpy as jnp
import numpy as np
from jax import lax
from jax.experimental import pallas as pl
from jax.experimental.pallas import tpu as pltpu
from jax.sharding import Mesh, PartitionSpec as P

X = ("xh", "xl")
EP = X + ("y", "c")
N_X, N_Y, N_C = 4, 4, 2
N_YC = N_Y * N_C
N_EP = N_X * N_YC
BLOCK = 24
TRADED = (80, 112)
COLUMNS = 512
VMEM_LIMIT = 60 << 20
CHEAP = pl.CostEstimate(flops=1000, bytes_accessed=1000, transcendentals=0)
HBM = pl.BlockSpec(memory_space=pltpu.HBM)
SMEM = pl.BlockSpec(memory_space=pltpu.SMEM)
WHOLE = pl.BlockSpec(memory_space=pltpu.VMEM)


def shifted(block, axis, distance):
    count = lax.axis_size(axis)
    return lax.ppermute(block, axis, [(i, (i + distance) % count) for i in range(count)])


TOKEN = jax.ShapeDtypeStruct((8, 128), jnp.float32)


def ordered_call(kernel, operands, after, out_shape, out_specs, scratch, in_specs=None, aliases=None):
    after = [t for t in after if t is not None]
    in_specs = in_specs or [HBM] * len(operands)

    def body(*refs):
        ins, rest = refs[: len(operands)], refs[len(operands) + len(after) :]
        kernel(*ins, *rest[: len(out_shape)], *rest[len(out_shape) + 1 :])

    *outs, token = pl.pallas_call(
        body,
        out_shape=list(out_shape) + [TOKEN],
        in_specs=list(in_specs) + [HBM] * len(after),
        out_specs=list(out_specs) + [HBM],
        scratch_shapes=scratch,
        input_output_aliases=aliases or {},
        compiler_params=pltpu.CompilerParams(vmem_limit_bytes=VMEM_LIMIT),
        cost_estimate=CHEAP,
    )(*operands, *after)
    return outs, token


def through(moves, reads, writes):
    reading = [pltpu.make_async_copy(m[0], m[1], reads.at[i]) for i, m in enumerate(moves)]
    writing = [pltpu.make_async_copy(m[1], m[2], writes.at[i]) for i, m in enumerate(moves)]
    for copy in reading:
        copy.start()
    for read, write in zip(reading, writing):
        read.wait()
        write.start()
    for copy in writing:
        copy.wait()


def cut_kernel(ranges, quarter, part, weight, *refs):
    count = len(ranges)
    outs, held, (reads, writes) = refs[:count], refs[count : 2 * count], refs[2 * count :]
    moves = []
    for out, stop, (at, rows) in zip(outs, held, ranges):
        start = pl.multiple_of(part[0] * quarter + at, 16)
        moves.append((weight.at[:, pl.ds(start, rows)], stop, out))
    through(moves, reads, writes)


def cut(part, weight, ranges, quarter, after):
    shapes = [(2, rows, weight.shape[2]) for _, rows in ranges]
    return ordered_call(
        functools.partial(cut_kernel, ranges, quarter),
        [part, weight],
        after,
        [jax.ShapeDtypeStruct(shape, weight.dtype) for shape in shapes],
        [HBM] * len(shapes),
        [pltpu.VMEM(shape, weight.dtype) for shape in shapes]
        + [pltpu.SemaphoreType.DMA((len(shapes),))] * 2,
        in_specs=[SMEM, HBM],
    )


def last_kernel(partner, weight, *refs):
    *refs, held, reads, writes = refs
    out = refs[(len(refs) - 1) // 2]
    rows = held.shape[1]
    first = weight.shape[1] - out.shape[0]
    moves = []
    for i in range(held.shape[0]):
        source = weight.at[partner[0], pl.ds(first + i * rows, rows)]
        moves.append((source, held.at[i], out.at[pl.ds(i * rows, rows)]))
    through(moves, reads, writes)


def last_rows(partner, weight, count, after, passed):
    shape = (count, weight.shape[2])
    return ordered_call(
        last_kernel,
        [partner, weight, *passed],
        after,
        [jax.ShapeDtypeStruct(shape, weight.dtype)]
        + [jax.ShapeDtypeStruct(p.shape, p.dtype) for p in passed],
        [HBM] * (1 + len(passed)),
        [pltpu.VMEM((4, count // 4, shape[1]), weight.dtype)]
        + [pltpu.SemaphoreType.DMA((4,))] * 2,
        in_specs=[SMEM, HBM] + [HBM] * len(passed),
        aliases={2 + i: 1 + i for i in range(len(passed))},
    )


def pick_kernel(others, picks, block, *refs):
    *refs, held, reads, writes = refs
    passed = (len(refs) - others) // 2
    outs = refs[passed : passed + others]
    through([(block.at[picks[i + 1]], held.at[i], o) for i, o in enumerate(outs)], reads, writes)


def pick(picks, block, parts, after, passed=()):
    others = parts - 1
    operands = [picks, block, *passed]
    return ordered_call(
        functools.partial(pick_kernel, others),
        operands,
        after,
        [jax.ShapeDtypeStruct(block.shape[1:], block.dtype)] * others
        + [jax.ShapeDtypeStruct(p.shape, p.dtype) for p in passed],
        [HBM] * (others + len(passed)),
        [pltpu.VMEM((others,) + block.shape[1:], block.dtype)]
        + [pltpu.SemaphoreType.DMA((others,))] * 2,
        in_specs=[SMEM] + [HBM] * (1 + len(passed)),
        aliases={2 + i: others + i for i in range(len(passed))},
    )


def place_kernel(at, quarter, parts, picks, part, block, *refs):
    *refs, held, reads, writes = refs
    arrived, out = refs[: parts - 1], refs[-1]
    rows = arrived[0].shape[0]
    moves = []
    for i, source in enumerate([block.at[picks[0]], *arrived]):
        origin = lax.rem(part[0] - i + parts, parts)
        start = pl.multiple_of(origin * quarter + at, 16)
        moves.append((source, held.at[i], out.at[0, pl.ds(start, rows)]))
    through(moves, reads, writes)


def placed(picks, part, block, arrived, at, quarter, depth, whole, after):
    parts = len(arrived) + 1
    rows, width = arrived[0].shape
    chained = whole is not None
    operands = [picks, part, block, *arrived] + ([whole] if chained else [])
    (whole,), token = ordered_call(
        functools.partial(place_kernel, at, quarter, parts),
        operands,
        after,
        [jax.ShapeDtypeStruct((1, depth, width), block.dtype)],
        [HBM],
        [pltpu.VMEM((parts, rows, width), block.dtype)]
        + [pltpu.SemaphoreType.DMA((parts,))] * 2,
        in_specs=[SMEM, SMEM] + [HBM] * (len(operands) - 2),
        aliases={len(operands) - 1: 0} if chained else {},
    )
    return whole, token


def direct_kernel(block, _, out, held, reads, writes):
    rows = block.shape[0] // 4
    through(
        [
            (
                block.at[pl.ds(i * rows, rows)],
                held.at[i],
                out.at[0, pl.ds(out.shape[1] - (4 - i) * rows, rows)],
            )
            for i in range(4)
        ],
        reads,
        writes,
    )


def placed_direct(block, whole, after):
    (whole,), token = ordered_call(
        direct_kernel,
        [block, whole],
        after,
        [jax.ShapeDtypeStruct(whole.shape, whole.dtype)],
        [HBM],
        [pltpu.VMEM((4, block.shape[0] // 4, block.shape[1]), block.dtype)]
        + [pltpu.SemaphoreType.DMA((4,))] * 2,
        aliases={1: 0},
    )
    return whole, token


def rank_of(expert_list):
    count = expert_list.shape[-1]
    order = jnp.arange(count, dtype=jnp.int32)
    same = expert_list[..., :, None] == expert_list[..., None, :]
    return jnp.sum(same & (order[:, None] > order[None, :]), axis=-1, dtype=jnp.int32)


def one_hot_rows(sources, count):
    table = np.zeros((len(sources), count), np.float32)
    table[np.arange(len(sources)), sources] = 1.0
    return table


STACK = N_X * 20


def return_order():
    rows, names = [], []
    for yc in range(N_YC):
        bases = [(x * N_YC + yc) * BLOCK for x in range(N_X)]
        for base in bases:
            rows += [base + r for r in range(8)]
            names += [base + 15] * 8
        for base in bases:
            for at in (base + 8, base + 16):
                rows += [at + r for r in range(6)]
                names += [at + 7] * 6
    return one_hot_rows(rows, N_EP * BLOCK), one_hot_rows(names, N_EP * BLOCK)


def scale_kernel(partner, scale, out):
    first = scale[0:1].astype(jnp.float32)
    second = scale[1:2].astype(jnp.float32)
    out[...] = jnp.where(partner[0] == 0, first, second).astype(out.dtype)


def chosen_scale(partner, scale, after):
    (chosen,), token = ordered_call(
        scale_kernel,
        [partner, scale],
        after,
        [jax.ShapeDtypeStruct((1, scale.shape[1]), scale.dtype)],
        [WHOLE],
        [],
        in_specs=[SMEM, WHOLE],
    )
    return chosen, token


def serve_kernel(me, received, order, naming, weight, scale, *refs):
    out, _, spread, held, product, reads, writes = refs[-7:]
    depth = received.shape[1]
    tiles = held.shape[0]
    columns = [pl.ds(i * COLUMNS, COLUMNS) for i in range(tiles)]
    reading = [
        pltpu.make_async_copy(weight.at[:, :, columns[i]], held.at[i], reads.at[i])
        for i in range(tiles)
    ]
    writing = [
        pltpu.make_async_copy(product.at[i], out.at[:, columns[i]], writes.at[i])
        for i in range(tiles)
    ]
    for copy in reading:
        copy.start()
    ordered = jnp.dot(order[...], received[...], preferred_element_type=jnp.float32)
    named = jnp.dot(naming[...], received[:, :128], preferred_element_type=jnp.float32)
    row = lax.broadcasted_iota(jnp.int32, named.shape, 0)
    lane = jnp.where(
        row % STACK < N_X * 8,
        ((row // 4) % 2).astype(jnp.float32),
        named - (2 * me[0]).astype(jnp.float32),
    )[:, 0:1]
    spread[:, :depth] = jnp.where(lane == 0.0, ordered, 0.0).astype(jnp.bfloat16)
    spread[:, depth:] = jnp.where(lane == 1.0, ordered, 0.0).astype(jnp.bfloat16)
    for i in range(tiles):
        reading[i].wait()
        both = held[i].reshape(2 * depth, COLUMNS)
        scales = scale[:, i * COLUMNS : (i + 1) * COLUMNS].astype(jnp.float32)
        total = jnp.dot(spread[...], both, preferred_element_type=jnp.float32)
        total = total * jnp.where(lane == 0.0, scales[0:1], scales[1:2])
        product[i] = total.astype(jnp.bfloat16)
        writing[i].start()
    for copy in writing:
        copy.wait()


def serve(me, received, weight, scale, after):
    order, naming = (jnp.asarray(table, jnp.bfloat16) for table in return_order())
    rows = order.shape[0]
    _, depth, width = weight.shape
    tiles = width // COLUMNS
    return pl.pallas_call(
        serve_kernel,
        in_specs=[SMEM, WHOLE, WHOLE, WHOLE, HBM, WHOLE] + [HBM] * len(after),
        out_specs=[HBM, HBM],
        scratch_shapes=[
            pltpu.VMEM((rows, 2 * depth), jnp.bfloat16),
            pltpu.VMEM((tiles, 2, depth, COLUMNS), jnp.bfloat16),
            pltpu.VMEM((tiles, rows, COLUMNS), jnp.bfloat16),
            pltpu.SemaphoreType.DMA((tiles,)),
            pltpu.SemaphoreType.DMA((tiles,)),
        ],
        out_shape=[jax.ShapeDtypeStruct((rows, width), jnp.bfloat16), TOKEN],
        compiler_params=pltpu.CompilerParams(vmem_limit_bytes=VMEM_LIMIT),
        cost_estimate=CHEAP,
    )(me, received, order, naming, weight, scale, *after)


def mixing(told, my_x, steps, rows, top):
    items = rows * top
    told = told.astype(jnp.float32).reshape(N_X, 4, steps, items)
    ids = told[:, 0].astype(jnp.int32)
    gates = told[:, 1] + told[:, 2] + told[:, 3]
    rank = rank_of(ids)
    who = jnp.arange(N_X * steps, dtype=jnp.int32).reshape(N_X, steps, 1) * 256
    code = jnp.where(rank < 2, ids * 2 + rank, 128 + rank - 2) + who
    source = jnp.arange(N_YC, dtype=jnp.int32)[:, None]
    row = jnp.arange(N_X * 8, dtype=jnp.int32)[None, :]
    slot_code = ((N_YC * my_x + source) * 2 + (row % 8) // 4) * 2 + row % 2
    slot_code = slot_code + ((row // 8) * steps + (row % 4) // 2) * 256
    row = jnp.arange(N_X * 12, dtype=jnp.int32)[None, :]
    hot_code = 128 + row % 6 + ((row // 12) * steps + (row % 12) // 6) * 256
    hot_code = jnp.broadcast_to(hot_code, (N_YC, N_X * 12))
    column_code = jnp.concatenate([slot_code, hot_code], 1).reshape(-1)
    code = code.reshape(N_X * steps * rows, top)
    gates = gates.reshape(N_X * steps * rows, top)
    mix = jnp.sum(
        jnp.where(code[:, :, None] == column_code[None, None, :], gates[:, :, None], 0.0), axis=1
    )
    high = lax.reduce_precision(mix, 8, 7)
    return jnp.concatenate([high, mix - high], 0).astype(jnp.bfloat16)


def mix_kernel(mixes, returned, out, held, product, reads, writes):
    tiles = held.shape[0]
    columns = [pl.ds(i * COLUMNS, COLUMNS) for i in range(tiles)]
    reading = [
        pltpu.make_async_copy(returned.at[:, columns[i]], held.at[i], reads.at[i])
        for i in range(tiles)
    ]
    writing = [
        pltpu.make_async_copy(product.at[i], out.at[:, columns[i]], writes.at[i])
        for i in range(tiles)
    ]
    for copy in reading:
        copy.start()
    many = out.shape[0]
    for i in range(tiles):
        reading[i].wait()
        total = jnp.dot(mixes[...], held[i], preferred_element_type=jnp.float32)
        product[i] = (total[:many] + total[many:]).astype(out.dtype)
        writing[i].start()
    for copy in writing:
        copy.wait()


def mixed(mixes, returned):
    rows, (many, width) = mixes.shape[0] // 2, returned.shape
    tiles = width // COLUMNS
    return pl.pallas_call(
        mix_kernel,
        in_specs=[WHOLE, HBM],
        out_specs=HBM,
        out_shape=jax.ShapeDtypeStruct((rows, width), jnp.bfloat16),
        scratch_shapes=[
            pltpu.VMEM((tiles, many, COLUMNS), jnp.bfloat16),
            pltpu.VMEM((tiles, rows, COLUMNS), jnp.bfloat16),
            pltpu.SemaphoreType.DMA((tiles,)),
            pltpu.SemaphoreType.DMA((tiles,)),
        ],
        compiler_params=pltpu.CompilerParams(vmem_limit_bytes=VMEM_LIMIT),
        cost_estimate=CHEAP,
    )(mixes, returned)


def local(hidden_in, expert_ids, gates, expert_weight, column_scale, replica_map):
    steps, rows, top, depth = hidden_in.shape
    width = expert_weight.shape[2]
    items = rows * top
    my_x, my_yc, me = lax.axis_index(X), lax.axis_index(("y", "c")), lax.axis_index(EP)

    expert_list = expert_ids.reshape(steps, items)
    rank = rank_of(expert_list)
    step_of = jnp.arange(steps, dtype=jnp.int32)[:, None]
    place = jnp.where(
        rank < 2,
        (expert_list // 2) * BLOCK + (expert_list % 2) * 4 + step_of * 2 + rank,
        1000 + step_of * 8 + rank - 2,
    ).reshape(steps * items)
    place = jnp.concatenate([place, jnp.array([1006, 1007, 1015, -1, -1, -1, -1, -1], jnp.int32)])
    line = jnp.arange(N_EP * BLOCK, dtype=jnp.int32)
    line = jnp.where(line % BLOCK < 8, line, 1000 + line % BLOCK - 8)
    selector = (line[:, None] == place[None, :]).astype(jnp.bfloat16)
    hot_id = jnp.sum(jnp.where(rank == 7, expert_list, 0), axis=1).astype(jnp.float32)
    flat_gates = gates.reshape(steps * items)
    high = lax.reduce_precision(flat_gates, 8, 7)
    middle = lax.reduce_precision(flat_gates - high, 8, 7)
    low = flat_gates - high - middle
    told = jnp.concatenate([expert_list.reshape(steps * items).astype(jnp.float32), high, middle, low])
    further = jnp.concatenate(
        [told[None], jnp.broadcast_to(hot_id[:, None], (steps, depth)), jnp.zeros((5, depth), jnp.float32)]
    ).astype(jnp.bfloat16)
    hidden = jnp.concatenate([hidden_in.reshape(steps * items, depth), further])
    part, parts = lax.axis_index("dp"), lax.axis_size("dp")
    here = part.reshape(1).astype(jnp.int32)
    quarter = sum(TRADED)
    starts = [sum(TRADED[:i]) for i in range(len(TRADED))]
    ranges = list(zip(starts, TRADED))
    partner = lax.dynamic_slice(replica_map, ((me + N_EP // 2) % N_EP,), (1,)) % 2
    blocks, token = cut(here, expert_weight, ranges, quarter, [])
    crossed = [shifted(block, "xh", 1) for block in blocks]

    outgoing = jnp.dot(selector, hidden, preferred_element_type=jnp.float32).astype(jnp.bfloat16)
    received = lax.all_to_all(outgoing.reshape(N_EP, BLOCK, depth), EP, 0, 0, tiled=True)
    mine = lax.dynamic_slice(replica_map, (me,), (1,)) % 2
    picks = lax.psum(jnp.where(jnp.arange(parts) == part, mine, 0), "dp")
    picks = jnp.roll(picks, -part)
    scale, _ = chosen_scale(partner, column_scale, [])
    replica_scale = shifted(scale, "xh", 1)

    def traded(j, after, passed=()):
        (*sent, last), token = pick(picks, crossed[j], parts, after, passed)
        if not passed:
            sent, last = sent + [last], None
        return [shifted(piece, "dp", d + 1) for d, piece in enumerate(sent)], last, token

    def put(j, pieces, whole, after):
        return placed(picks, here, crossed[j], pieces, starts[j], quarter, depth, whole, after)

    received = received.reshape(N_EP * BLOCK, depth)
    where = me.reshape(1).astype(jnp.int32)
    returned, token = serve(where, received, expert_weight, column_scale, [token, picks])
    told = received.reshape(N_X, N_YC, BLOCK, depth)[:, :, 14]
    told = lax.dynamic_index_in_dim(told, my_yc, 1, keepdims=False)
    first, returned, token = traded(0, [token, replica_scale], [returned])
    returned = lax.all_to_all(returned.reshape(N_YC, -1, width), ("y", "c"), 0, 0, tiled=True)
    whole, token = put(0, first, None, [token])
    (direct, told), token = last_rows(
        partner, expert_weight, depth - parts * quarter, [token], [told]
    )
    direct = shifted(direct, "xh", 1)
    second, _, token = traded(1, [token])
    whole, token = put(1, second, whole, [token])
    replica_weight, token = placed_direct(direct, whole, [token])

    mixes = mixing(told, my_x, steps, rows, top)
    partial = mixed(mixes, returned.reshape(-1, width))
    partial = lax.all_to_all(partial.reshape(N_X, steps * rows, width), X, 0, 0, tiled=True)
    combined = jnp.sum(partial.astype(jnp.float32), axis=0).astype(jnp.bfloat16)
    return combined.reshape(steps, rows, width), replica_weight, replica_scale


def solution(mesh):
    grid = Mesh(mesh.devices.reshape(-1, 2, N_X // 2, N_Y, N_C), ("dp",) + EP)
    everywhere = ("dp",) + EP
    in_specs = (
        P(None, everywhere, None, None),
        P(None, everywhere, None),
        P(None, everywhere, None),
        P(EP, None, None),
        P(EP, None),
        P("dp"),
    )
    out_specs = (P(None, everywhere, None), P(everywhere, None, None), P(everywhere, None))
    return jax.shard_map(local, mesh=grid, in_specs=in_specs, out_specs=out_specs, check_vma=False)
```

```python
import functools

import jax
import jax.numpy as jnp
import numpy as np
from jax import lax
from jax.experimental import pallas as pl
from jax.experimental.pallas import tpu as pltpu
from jax.sharding import Mesh, PartitionSpec as P

X = ("xh", "xl")
EP = X + ("y", "c")
N_X, N_Y, N_C = 4, 4, 2
N_YC = N_Y * N_C
N_EP = N_X * N_YC
BLOCK = 16
TRADED = (64, 128)
COLUMNS = 512
VMEM_LIMIT = 60 << 20
AHEAD = 3
CHEAP = pl.CostEstimate(flops=1000, bytes_accessed=1000, transcendentals=0)
HBM = pl.BlockSpec(memory_space=pltpu.HBM)
ANY = pl.BlockSpec(memory_space=pl.ANY)
SMEM = pl.BlockSpec(memory_space=pltpu.SMEM)
WHOLE = pl.BlockSpec(memory_space=pltpu.VMEM)


def shifted(block, axis, distance):
    count = lax.axis_size(axis)
    return lax.ppermute(block, axis, [(i, (i + distance) % count) for i in range(count)])


TOKEN = jax.ShapeDtypeStruct((8, 128), jnp.float32)


def ordered_call(kernel, operands, after, out_shape, out_specs, scratch, in_specs=None, aliases=None, limit=60):
    after = [t for t in after if t is not None]
    in_specs = in_specs or [HBM] * len(operands)

    def body(*refs):
        ins, rest = refs[: len(operands)], refs[len(operands) + len(after) :]
        kernel(*ins, *rest[: len(out_shape)], *rest[len(out_shape) + 1 :])

    *outs, token = pl.pallas_call(
        body,
        out_shape=list(out_shape) + [TOKEN],
        in_specs=list(in_specs) + [HBM] * len(after),
        out_specs=list(out_specs) + [HBM],
        scratch_shapes=scratch,
        input_output_aliases=aliases or {},
        compiler_params=pltpu.CompilerParams(vmem_limit_bytes=limit << 20),
        cost_estimate=CHEAP,
    )(*operands, *after)
    return outs, token


def through(moves, reads, writes):
    reading = [pltpu.make_async_copy(m[0], m[1], reads.at[i]) for i, m in enumerate(moves)]
    writing = [pltpu.make_async_copy(m[1], m[2], writes.at[i]) for i, m in enumerate(moves)]
    for copy in reading:
        copy.start()
    for read, write in zip(reading, writing):
        read.wait()
        write.start()
    for copy in writing:
        copy.wait()


def cut_kernel(ranges, quarter, part, weight, *refs):
    count = len(ranges)
    outs, held, (reads, writes) = refs[:count], refs[count : 2 * count], refs[2 * count :]
    moves = []
    for out, stop, (at, rows) in zip(outs, held, ranges):
        start = pl.multiple_of(part[0] * quarter + at, 16)
        moves.append((weight.at[:, pl.ds(start, rows)], stop, out))
    through(moves, reads, writes)


def cut(part, weight, ranges, quarter, after):
    shapes = [(2, rows, weight.shape[2]) for _, rows in ranges]
    return ordered_call(
        functools.partial(cut_kernel, ranges, quarter),
        [part, weight],
        after,
        [jax.ShapeDtypeStruct(shape, weight.dtype) for shape in shapes],
        [HBM] * len(shapes),
        [pltpu.VMEM(shape, weight.dtype) for shape in shapes]
        + [pltpu.SemaphoreType.DMA((len(shapes),))] * 2,
        in_specs=[SMEM, HBM],
    )


def last_kernel(partner, weight, out, held, reads, writes):
    rows = held.shape[1]
    first = weight.shape[1] - out.shape[0]
    moves = []
    for i in range(held.shape[0]):
        source = weight.at[partner[0], pl.ds(first + i * rows, rows)]
        moves.append((source, held.at[i], out.at[pl.ds(i * rows, rows)]))
    through(moves, reads, writes)


def last_rows(partner, weight, count, after):
    shape = (count, weight.shape[2])
    (rows,), token = ordered_call(
        last_kernel,
        [partner, weight],
        after,
        [jax.ShapeDtypeStruct(shape, weight.dtype)],
        [HBM],
        [pltpu.VMEM((4, count // 4, shape[1]), weight.dtype)]
        + [pltpu.SemaphoreType.DMA((4,))] * 2,
        in_specs=[SMEM, HBM],
    )
    return rows, token


def pick_kernel(picks, block, *refs):
    *outs, held, reads, writes = refs
    through([(block.at[picks[i + 1]], held.at[i], o) for i, o in enumerate(outs)], reads, writes)


def pick(picks, block, parts, after):
    others = parts - 1
    return ordered_call(
        pick_kernel,
        [picks, block],
        after,
        [jax.ShapeDtypeStruct(block.shape[1:], block.dtype)] * others,
        [HBM] * others,
        [pltpu.VMEM((others,) + block.shape[1:], block.dtype)]
        + [pltpu.SemaphoreType.DMA((others,))] * 2,
        in_specs=[SMEM, ANY],
        limit=12,
    )


def gate_kernel(*_):
    pass


def gated(passed, after):
    (passed,), _ = ordered_call(
        gate_kernel,
        [passed],
        after,
        [jax.ShapeDtypeStruct(passed.shape, passed.dtype)],
        [HBM],
        [],
        aliases={0: 0},
    )
    return passed


def place_kernel(at, quarter, parts, picks, part, block, *refs):
    *refs, out, held, reads, writes = refs
    arrived = refs[: parts - 1]
    rows = arrived[0].shape[0]
    moves = []
    for i, source in enumerate([block.at[picks[0]], *arrived]):
        origin = lax.rem(part[0] - i + parts, parts)
        start = pl.multiple_of(origin * quarter + at, 16)
        moves.append((source, held.at[i], out.at[0, pl.ds(start, rows)]))
    through(moves, reads, writes)


def placed(picks, part, block, arrived, at, quarter, depth, whole, after):
    parts = len(arrived) + 1
    rows, width = arrived[0].shape
    chained = whole is not None
    operands = [picks, part, block, *arrived] + ([whole] if chained else [])
    (whole,), token = ordered_call(
        functools.partial(place_kernel, at, quarter, parts),
        operands,
        after,
        [jax.ShapeDtypeStruct((1, depth, width), block.dtype)],
        [HBM],
        [pltpu.VMEM((parts, rows, width), block.dtype)]
        + [pltpu.SemaphoreType.DMA((parts,))] * 2,
        in_specs=[SMEM, SMEM] + [ANY] * parts + [HBM] * chained,
        aliases={len(operands) - 1: 0} if chained else {},
        limit=12,
    )
    return whole, token


def finish_kernel(at, quarter, parts, picks, part, block, *refs):
    arrived, (straight, _, out, held, rest, reads, writes) = refs[: parts - 1], refs[parts - 1 :]
    rows = arrived[0].shape[0]
    moves = []
    share = rest.shape[1]
    for i in range(parts):
        first = out.shape[1] - (parts - i) * share
        moves.append(
            (straight.at[pl.ds(i * share, share)], rest.at[i], out.at[0, pl.ds(first, share)])
        )
    for i, source in enumerate([block.at[picks[0]], *arrived]):
        origin = lax.rem(part[0] - i + parts, parts)
        start = pl.multiple_of(origin * quarter + at, 16)
        moves.append((source, held.at[i], out.at[0, pl.ds(start, rows)]))
    through(moves, reads, writes)


def finished(picks, part, block, arrived, straight, at, quarter, whole, after):
    parts = len(arrived) + 1
    rows, width = arrived[0].shape
    operands = [picks, part, block, *arrived, straight, whole]
    (whole,), _ = ordered_call(
        functools.partial(finish_kernel, at, quarter, parts),
        operands,
        after,
        [jax.ShapeDtypeStruct(whole.shape, block.dtype)],
        [HBM],
        [
            pltpu.VMEM((parts, rows, width), block.dtype),
            pltpu.VMEM((parts, straight.shape[0] // parts, width), block.dtype),
        ]
        + [pltpu.SemaphoreType.DMA((2 * parts,))] * 2,
        in_specs=[SMEM, SMEM] + [ANY] * (parts + 1) + [HBM],
        aliases={len(operands) - 1: 0},
        limit=16,
    )
    return whole


def rank_of(expert_list):
    count = expert_list.shape[-1]
    order = jnp.arange(count, dtype=jnp.int32)
    same = expert_list[..., :, None] == expert_list[..., None, :]
    return jnp.sum(same & (order[:, None] > order[None, :]), axis=-1, dtype=jnp.int32)


STACK = N_X * 20


def one_hot_rows(sources):
    table = np.zeros((len(sources), N_EP * (BLOCK + 8)), np.float32)
    table[np.arange(len(sources)), sources] = 1.0
    return table


def return_order():
    orders, namings = [], []
    for core in range(N_C):
        rows, names = [], []
        for yc in range(N_YC):
            clients = [x * N_YC + yc for x in range(N_X)]
            for client in clients:
                rows += [client * BLOCK + r for r in range(8)]
                names += [client * BLOCK + 15] * 8
            for client in clients:
                for step in range(2):
                    at = client * BLOCK + 8 if step == core else N_EP * BLOCK + client * 8
                    rows += [at + r for r in range(6)]
                    names += [at + 7] * 6
        orders.append(one_hot_rows(rows))
        namings.append(one_hot_rows(names))
    return np.stack([np.stack(orders), np.stack(namings)], 1)


def scale_kernel(partner, scale, out):
    first = scale[0:1].astype(jnp.float32)
    second = scale[1:2].astype(jnp.float32)
    out[...] = jnp.where(partner[0] == 0, first, second).astype(out.dtype)


def chosen_scale(partner, scale, after):
    (chosen,), token = ordered_call(
        scale_kernel,
        [partner, scale],
        after,
        [jax.ShapeDtypeStruct((1, scale.shape[1]), scale.dtype)],
        [WHOLE],
        [],
        in_specs=[SMEM, WHOLE],
    )
    return chosen, token


def serve_kernel(me, received, far, order, weight, scale, *refs):
    out, _, table, spread, held, product, table_read, reads, writes = refs[-9:]
    near, depth = received.shape
    tiles = held.shape[0]
    columns = [pl.ds(i * COLUMNS, COLUMNS) for i in range(tiles)]
    table_reading = pltpu.make_async_copy(order.at[me[1]], table, table_read)
    reading = [
        pltpu.make_async_copy(weight.at[:, :, columns[i]], held.at[i], reads.at[i])
        for i in range(tiles)
    ]
    writing = [
        pltpu.make_async_copy(product.at[i], out.at[:, columns[i]], writes.at[i])
        for i in range(tiles)
    ]
    table_reading.start()
    table_reading.wait()
    for copy in reading[:AHEAD]:
        copy.start()

    def gather(which, first, second):
        rows = jnp.dot(table[which, :, :near], first, preferred_element_type=jnp.float32)
        return rows + jnp.dot(table[which, :, near:], second, preferred_element_type=jnp.float32)

    ordered = gather(0, received[...], far[...])
    named = gather(1, received[:, :128], far[:, :128])
    row = lax.broadcasted_iota(jnp.int32, named.shape, 0)
    lane = jnp.where(
        row % STACK < N_X * 8,
        ((row // 4) % 2).astype(jnp.float32),
        named - (2 * me[0]).astype(jnp.float32),
    )[:, 0:1]
    spread[:, :depth] = jnp.where(lane == 0.0, ordered, 0.0).astype(jnp.bfloat16)
    spread[:, depth:] = jnp.where(lane == 1.0, ordered, 0.0).astype(jnp.bfloat16)
    for i in range(tiles):
        reading[i].wait()
        if i + AHEAD < tiles:
            reading[i + AHEAD].start()
        both = held[i].reshape(2 * depth, COLUMNS)
        scales = scale[:, i * COLUMNS : (i + 1) * COLUMNS].astype(jnp.float32)
        total = jnp.dot(spread[...], both, preferred_element_type=jnp.float32)
        total = total * jnp.where(lane == 0.0, scales[0:1], scales[1:2])
        product[i] = total.astype(jnp.bfloat16)
        writing[i].start()
    for copy in writing:
        copy.wait()


def serve(me, received, far, weight, scale, after):
    order = jnp.asarray(return_order(), jnp.bfloat16)
    rows = order.shape[2]
    _, depth, width = weight.shape
    tiles = width // COLUMNS
    return pl.pallas_call(
        serve_kernel,
        in_specs=[SMEM, WHOLE, WHOLE, HBM, HBM, WHOLE] + [HBM] * len(after),
        out_specs=[HBM, HBM],
        scratch_shapes=[
            pltpu.VMEM(order.shape[1:], jnp.bfloat16),
            pltpu.VMEM((rows, 2 * depth), jnp.bfloat16),
            pltpu.VMEM((tiles, 2, depth, COLUMNS), jnp.bfloat16),
            pltpu.VMEM((tiles, rows, COLUMNS), jnp.bfloat16),
            pltpu.SemaphoreType.DMA,
            pltpu.SemaphoreType.DMA((tiles,)),
            pltpu.SemaphoreType.DMA((tiles,)),
        ],
        out_shape=[jax.ShapeDtypeStruct((rows, width), jnp.bfloat16), TOKEN],
        compiler_params=pltpu.CompilerParams(vmem_limit_bytes=VMEM_LIMIT),
        cost_estimate=CHEAP,
    )(me, received, far, order, weight, scale, *after)


def column_codes():
    codes, slots = [], []
    for source in range(N_YC):
        for x in range(N_X):
            for r in range(8):
                slot = (source * 2 + r // 4) * 2 + r % 2
                codes.append((x * 2 + r % 4 // 2) * 256 + slot)
                slots.append(1)
        for x in range(N_X):
            for r in range(12):
                codes.append((x * 2 + r // 6) * 256 + 128 + r % 6)
                slots.append(0)
    return np.array([codes], np.float32), np.array([slots], np.float32)


def mixing_kernel(told, columns, out):
    count = told.shape[2]
    tokens = out.shape[0] // 2 // (N_X * 2)
    row = lax.broadcasted_iota(jnp.int32, (count, count), 0)
    line = lax.broadcasted_iota(jnp.int32, (count, count), 1)
    token = lax.broadcasted_iota(jnp.int32, (tokens, count), 0)
    item = lax.broadcasted_iota(jnp.int32, (tokens, count), 1)
    mine = item // (count // tokens) == token
    for x in range(N_X):
        for step in range(2):
            ids = told[x, step : step + 1, :]
            down = jnp.sum(jnp.where(row == line, ids, 0.0), axis=1, keepdims=True)
            before = jnp.where((down == ids) & (line < row), 1.0, 0.0)
            rank = jnp.sum(before, axis=1, keepdims=True)
            code = jnp.where(rank < 2.0, down * 2.0 + rank, 126.0 + rank)
            code = code + float((x * 2 + step) * 256)
            slot = jnp.where(code == columns[...], 1.0, 0.0).astype(jnp.bfloat16)
            high = told[x, 2 + step : 3 + step, :]
            rest = told[x, 4 + step : 5 + step, :] + told[x, 6 + step : 7 + step, :]
            at = (x * 2 + step) * tokens
            for first, part in ((0, high), (out.shape[0] // 2, rest)):
                gate = jnp.where(mine, part, 0.0).astype(jnp.bfloat16)
                mix = jnp.dot(gate, slot, preferred_element_type=jnp.float32)
                out[first + at : first + at + tokens] = mix.astype(jnp.bfloat16)


def mixing(told, my_x, steps, rows, after):
    codes, slots = column_codes()
    columns = jnp.asarray(codes) + jnp.asarray(slots) * (my_x * N_YC * 4).astype(jnp.float32)
    told = told.astype(jnp.float32).reshape(N_X, 4 * steps, -1)
    (mixes,), token = ordered_call(
        mixing_kernel,
        [told, columns],
        after,
        [jax.ShapeDtypeStruct((2 * N_X * steps * rows, codes.shape[1]), jnp.bfloat16)],
        [WHOLE],
        [],
        in_specs=[WHOLE, WHOLE],
    )
    return mixes, token


def mix_kernel(mixes, returned, out, held, product, reads, writes):
    tiles = held.shape[0]
    columns = [pl.ds(i * COLUMNS, COLUMNS) for i in range(tiles)]
    reading = [
        pltpu.make_async_copy(returned.at[:, columns[i]], held.at[i], reads.at[i])
        for i in range(tiles)
    ]
    writing = [
        pltpu.make_async_copy(product.at[i], out.at[:, columns[i]], writes.at[i])
        for i in range(tiles)
    ]
    for copy in reading:
        copy.start()
    many = out.shape[0]
    for i in range(tiles):
        reading[i].wait()
        total = jnp.dot(mixes[...], held[i], preferred_element_type=jnp.float32)
        product[i] = (total[:many] + total[many:]).astype(out.dtype)
        writing[i].start()
    for copy in writing:
        copy.wait()


def mixed(mixes, returned):
    rows, (many, width) = mixes.shape[0] // 2, returned.shape
    tiles = width // COLUMNS
    return pl.pallas_call(
        mix_kernel,
        in_specs=[WHOLE, HBM],
        out_specs=HBM,
        out_shape=jax.ShapeDtypeStruct((rows, width), jnp.bfloat16),
        scratch_shapes=[
            pltpu.VMEM((tiles, many, COLUMNS), jnp.bfloat16),
            pltpu.VMEM((tiles, rows, COLUMNS), jnp.bfloat16),
            pltpu.SemaphoreType.DMA((tiles,)),
            pltpu.SemaphoreType.DMA((tiles,)),
        ],
        compiler_params=pltpu.CompilerParams(vmem_limit_bytes=VMEM_LIMIT),
        cost_estimate=CHEAP,
    )(mixes, returned)


def local(hidden_in, expert_ids, gates, expert_weight, column_scale, replica_map):
    steps, rows, top, depth = hidden_in.shape
    width = expert_weight.shape[2]
    items = rows * top
    my_x, my_yc, me = lax.axis_index(X), lax.axis_index(("y", "c")), lax.axis_index(EP)

    expert_list = expert_ids.reshape(steps, items)
    rank = rank_of(expert_list)
    step_of = jnp.arange(steps, dtype=jnp.int32)[:, None]
    place = jnp.where(
        rank < 2,
        (expert_list // 2) * BLOCK + (expert_list % 2) * 4 + step_of * 2 + rank,
        1000 + step_of * 8 + rank - 2,
    ).reshape(steps * items)
    extra = jnp.array([2006, 1007, 1015, -1, -1, -1, -1, -1], jnp.int32)
    place = jnp.concatenate([place, extra])
    line = jnp.arange(N_EP * BLOCK, dtype=jnp.int32)
    of_step = (line // BLOCK) % N_C * 8 + line % 8
    line = jnp.where(line % BLOCK < 8, line, jnp.where(line % 8 == 6, 2006, 1000 + of_step))
    selector = (line[:, None] == place[None, :]).astype(jnp.bfloat16)
    hot_id = jnp.sum(jnp.where(rank == 7, expert_list, 0), axis=1).astype(jnp.float32)
    flat_gates = gates.reshape(steps * items)
    high = lax.reduce_precision(flat_gates, 8, 7)
    middle = lax.reduce_precision(flat_gates - high, 8, 7)
    low = flat_gates - high - middle
    told = jnp.concatenate([expert_list.reshape(steps * items).astype(jnp.float32), high, middle, low])
    further = jnp.concatenate(
        [told[None], jnp.broadcast_to(hot_id[:, None], (steps, depth)), jnp.zeros((5, depth), jnp.float32)]
    ).astype(jnp.bfloat16)
    hidden = jnp.concatenate([hidden_in.reshape(steps * items, depth), further])
    part, parts = lax.axis_index("dp"), lax.axis_size("dp")
    here = part.reshape(1).astype(jnp.int32)
    quarter = sum(TRADED)
    starts = [sum(TRADED[:i]) for i in range(len(TRADED))]
    ranges = list(zip(starts, TRADED))
    partner = lax.dynamic_slice(replica_map, ((me + N_EP // 2) % N_EP,), (1,)) % 2
    outgoing = jnp.dot(selector, hidden, preferred_element_type=jnp.float32).astype(jnp.bfloat16)
    received = lax.all_to_all(outgoing.reshape(N_EP, BLOCK, depth), EP, 0, 0, tiled=True)
    mine = lax.dynamic_slice(replica_map, (me,), (1,)) % 2
    picks = lax.psum(jnp.where(jnp.arange(parts) == part, mine, 0), "dp")
    picks = jnp.roll(picks, -part)
    scale, token = chosen_scale(partner, column_scale, [picks])
    blocks, token = cut(here, expert_weight, ranges, quarter, [picks, token])
    replica_scale = shifted(scale, "xh", 1)

    def traded(j, after):
        sent, token = pick(picks, crossed[j], parts, after)
        return [shifted(piece, "dp", d + 1) for d, piece in enumerate(sent)], token

    far = shifted(received[:, 8:].reshape(N_EP * 8, depth), "c", 1)
    received = received.reshape(N_EP * BLOCK, depth)
    blocks[0] = gated(blocks[0], [received])
    crossed = [shifted(block, "xh", 1) for block in blocks]
    where = jnp.stack([me, lax.axis_index("c")]).astype(jnp.int32)
    returned, token = serve(where, received, far, expert_weight, column_scale, [token, picks])
    told = received.reshape(N_X, N_YC, BLOCK, depth)[:, :, 14]
    told = lax.dynamic_index_in_dim(told, my_yc, 1, keepdims=False)
    returned = gated(returned, [crossed[0], replica_scale])
    returned = lax.all_to_all(returned.reshape(N_YC, -1, width), ("y", "c"), 0, 0, tiled=True)
    first, token = traded(0, [token])
    mixes, token = mixing(told, my_x, steps, rows, [token])
    straight, token = last_rows(
        partner, expert_weight, depth - parts * quarter, [token, *first]
    )
    straight = shifted(straight, "xh", 1)
    whole, token = placed(
        picks, here, crossed[0], first, starts[0], quarter, depth, None, [token]
    )
    second, token = traded(1, [token])
    replica_weight = finished(
        picks, here, crossed[1], second, straight, starts[1], quarter, whole, [token]
    )

    partial = mixed(mixes, returned.reshape(-1, width))
    partial = lax.all_to_all(partial.reshape(N_X, steps * rows, width), X, 0, 0, tiled=True)
    combined = jnp.sum(partial.astype(jnp.float32), axis=0).astype(jnp.bfloat16)
    return combined.reshape(steps, rows, width), replica_weight, replica_scale


def solution(mesh):
    grid = Mesh(mesh.devices.reshape(-1, 2, N_X // 2, N_Y, N_C), ("dp",) + EP)
    everywhere = ("dp",) + EP
    in_specs = (
        P(None, everywhere, None, None),
        P(None, everywhere, None),
        P(None, everywhere, None),
        P(EP, None, None),
        P(EP, None),
        P("dp"),
    )
    out_specs = (P(None, everywhere, None), P(everywhere, None, None), P(everywhere, None))
    return jax.shard_map(local, mesh=grid, in_specs=in_specs, out_specs=out_specs, check_vma=False)
```

```python
import functools

import jax
import jax.numpy as jnp
import numpy as np
from jax import lax
from jax.experimental import pallas as pl
from jax.experimental.pallas import tpu as pltpu
from jax.sharding import Mesh, PartitionSpec as P

X = ("xh", "xl")
EP = X + ("y", "c")
N_X, N_Y, N_C = 4, 4, 2
N_YC = N_Y * N_C
N_EP = N_X * N_YC
BLOCK = 16
TRADED = (64, 128)
COLUMNS = 512
VMEM_LIMIT = 50 << 20
AHEAD = 3
CHEAP = pl.CostEstimate(flops=1000, bytes_accessed=1000, transcendentals=0)
HBM = pl.BlockSpec(memory_space=pltpu.HBM)
ANY = pl.BlockSpec(memory_space=pl.ANY)
SMEM = pl.BlockSpec(memory_space=pltpu.SMEM)
WHOLE = pl.BlockSpec(memory_space=pltpu.VMEM)


def shifted(block, axis, distance):
    count = lax.axis_size(axis)
    return lax.ppermute(block, axis, [(i, (i + distance) % count) for i in range(count)])


TOKEN = jax.ShapeDtypeStruct((8, 128), jnp.float32)


def ordered_call(kernel, operands, after, out_shape, out_specs, scratch, in_specs=None, aliases=None, limit=50):
    after = [t for t in after if t is not None]
    in_specs = in_specs or [HBM] * len(operands)

    def body(*refs):
        ins, rest = refs[: len(operands)], refs[len(operands) + len(after) :]
        kernel(*ins, *rest[: len(out_shape)], *rest[len(out_shape) + 1 :])

    *outs, token = pl.pallas_call(
        body,
        out_shape=list(out_shape) + [TOKEN],
        in_specs=list(in_specs) + [HBM] * len(after),
        out_specs=list(out_specs) + [HBM],
        scratch_shapes=scratch,
        input_output_aliases=aliases or {},
        compiler_params=pltpu.CompilerParams(vmem_limit_bytes=limit << 20),
        cost_estimate=CHEAP,
    )(*operands, *after)
    return outs, token


def through(moves, reads, writes):
    reading = [pltpu.make_async_copy(m[0], m[1], reads.at[i]) for i, m in enumerate(moves)]
    writing = [pltpu.make_async_copy(m[1], m[2], writes.at[i]) for i, m in enumerate(moves)]
    for copy in reading:
        copy.start()
    for read, write in zip(reading, writing):
        read.wait()
        write.start()
    for copy in writing:
        copy.wait()


def cut_kernel(ranges, quarter, part, weight, *refs):
    count = len(ranges)
    outs, held, (reads, writes) = refs[:count], refs[count : 2 * count], refs[2 * count :]
    moves = []
    for out, stop, (at, rows) in zip(outs, held, ranges):
        start = pl.multiple_of(part[0] * quarter + at, 16)
        moves.append((weight.at[:, pl.ds(start, rows)], stop, out))
    through(moves, reads, writes)


def cut(part, weight, ranges, quarter, after):
    shapes = [(2, rows, weight.shape[2]) for _, rows in ranges]
    return ordered_call(
        functools.partial(cut_kernel, ranges, quarter),
        [part, weight],
        after,
        [jax.ShapeDtypeStruct(shape, weight.dtype) for shape in shapes],
        [HBM] * len(shapes),
        [pltpu.VMEM(shape, weight.dtype) for shape in shapes]
        + [pltpu.SemaphoreType.DMA((len(shapes),))] * 2,
        in_specs=[SMEM, HBM],
        limit=60,
    )


def last_kernel(partner, weight, out, held, reads, writes):
    rows = held.shape[1]
    first = weight.shape[1] - out.shape[0]
    moves = []
    for i in range(held.shape[0]):
        source = weight.at[partner[0], pl.ds(first + i * rows, rows)]
        moves.append((source, held.at[i], out.at[pl.ds(i * rows, rows)]))
    through(moves, reads, writes)


def last_rows(partner, weight, count, after):
    shape = (count, weight.shape[2])
    (rows,), token = ordered_call(
        last_kernel,
        [partner, weight],
        after,
        [jax.ShapeDtypeStruct(shape, weight.dtype)],
        [HBM],
        [pltpu.VMEM((4, count // 4, shape[1]), weight.dtype)]
        + [pltpu.SemaphoreType.DMA((4,))] * 2,
        in_specs=[SMEM, HBM],
    )
    return rows, token


def pick_kernel(picks, block, *refs):
    *outs, held, reads, writes = refs
    through([(block.at[picks[i + 1]], held.at[i], o) for i, o in enumerate(outs)], reads, writes)


def pick(picks, block, parts, after):
    others = parts - 1
    return ordered_call(
        pick_kernel,
        [picks, block],
        after,
        [jax.ShapeDtypeStruct(block.shape[1:], block.dtype)] * others,
        [HBM] * others,
        [pltpu.VMEM((others,) + block.shape[1:], block.dtype)]
        + [pltpu.SemaphoreType.DMA((others,))] * 2,
        in_specs=[SMEM, ANY],
        limit=12,
    )


def gate_kernel(*_):
    pass


def gated(passed, after):
    (passed,), _ = ordered_call(
        gate_kernel,
        [passed],
        after,
        [jax.ShapeDtypeStruct(passed.shape, passed.dtype)],
        [HBM],
        [],
        aliases={0: 0},
    )
    return passed


def place_kernel(at, quarter, parts, picks, part, block, *refs):
    *refs, out, held, reads, writes = refs
    arrived = refs[: parts - 1]
    rows = arrived[0].shape[0]
    moves = []
    for i, source in enumerate([block.at[picks[0]], *arrived]):
        origin = lax.rem(part[0] - i + parts, parts)
        start = pl.multiple_of(origin * quarter + at, 16)
        moves.append((source, held.at[i], out.at[0, pl.ds(start, rows)]))
    through(moves, reads, writes)


def placed(picks, part, block, arrived, at, quarter, depth, whole, after):
    parts = len(arrived) + 1
    rows, width = arrived[0].shape
    chained = whole is not None
    operands = [picks, part, block, *arrived] + ([whole] if chained else [])
    (whole,), token = ordered_call(
        functools.partial(place_kernel, at, quarter, parts),
        operands,
        after,
        [jax.ShapeDtypeStruct((1, depth, width), block.dtype)],
        [HBM],
        [pltpu.VMEM((parts, rows, width), block.dtype)]
        + [pltpu.SemaphoreType.DMA((parts,))] * 2,
        in_specs=[SMEM, SMEM] + [ANY] * parts + [HBM] * chained,
        aliases={len(operands) - 1: 0} if chained else {},
        limit=12,
    )
    return whole, token


def own_kernel(at, quarter, picks, part, block, straight, _, out, held, rest, reads, writes):
    rows, share = held.shape[0], rest.shape[1]
    count = rest.shape[0]
    start = pl.multiple_of(part[0] * quarter + at, 16)
    moves = [(block.at[picks[0]], held, out.at[0, pl.ds(start, rows)])]
    for i in range(count):
        first = out.shape[1] - (count - i) * share
        moves.append(
            (straight.at[pl.ds(i * share, share)], rest.at[i], out.at[0, pl.ds(first, share)])
        )
    through(moves, reads, writes)


def placed_own(picks, part, block, straight, at, quarter, whole, after):
    _, rows, width = block.shape
    (whole,), token = ordered_call(
        functools.partial(own_kernel, at, quarter),
        [picks, part, block, straight, whole],
        after,
        [jax.ShapeDtypeStruct(whole.shape, whole.dtype)],
        [HBM],
        [
            pltpu.VMEM((rows, width), block.dtype),
            pltpu.VMEM((4, straight.shape[0] // 4, width), block.dtype),
        ]
        + [pltpu.SemaphoreType.DMA((5,))] * 2,
        in_specs=[SMEM, SMEM, ANY, ANY, HBM],
        aliases={4: 0},
        limit=16,
    )
    return whole, token


def others_kernel(at, quarter, part, *refs):
    *arrived, _, out, held, reads, writes = refs
    parts = len(arrived) + 1
    rows = arrived[0].shape[0]
    moves = []
    for i, source in enumerate(arrived):
        origin = lax.rem(part[0] - i - 1 + parts, parts)
        start = pl.multiple_of(origin * quarter + at, 16)
        moves.append((source, held.at[i], out.at[0, pl.ds(start, rows)]))
    through(moves, reads, writes)


def placed_others(part, arrived, at, quarter, whole, after):
    rows, width = arrived[0].shape
    count = len(arrived)
    (whole,), _ = ordered_call(
        functools.partial(others_kernel, at, quarter),
        [part, *arrived, whole],
        after,
        [jax.ShapeDtypeStruct(whole.shape, whole.dtype)],
        [HBM],
        [pltpu.VMEM((count, rows, width), whole.dtype)]
        + [pltpu.SemaphoreType.DMA((count,))] * 2,
        in_specs=[SMEM] + [ANY] * count + [HBM],
        aliases={1 + count: 0},
        limit=16,
    )
    return whole


def rank_of(expert_list):
    count = expert_list.shape[-1]
    order = jnp.arange(count, dtype=jnp.int32)
    same = expert_list[..., :, None] == expert_list[..., None, :]
    return jnp.sum(same & (order[:, None] > order[None, :]), axis=-1, dtype=jnp.int32)


STACK = N_X * 20


def one_hot_rows(sources):
    table = np.zeros((len(sources), N_EP * (BLOCK + 8)), np.float32)
    table[np.arange(len(sources)), sources] = 1.0
    return table


def return_order():
    orders, namings = [], []
    for core in range(N_C):
        rows, names = [], []
        for yc in range(N_YC):
            clients = [x * N_YC + yc for x in range(N_X)]
            for client in clients:
                rows += [client * BLOCK + r for r in range(8)]
                names += [client * BLOCK + 15] * 8
            for client in clients:
                for step in range(2):
                    at = client * BLOCK + 8 if step == core else N_EP * BLOCK + client * 8
                    rows += [at + r for r in range(6)]
                    names += [at + 7] * 6
        orders.append(one_hot_rows(rows))
        namings.append(one_hot_rows(names))
    return np.stack([np.stack(orders), np.stack(namings)], 1)


def scale_kernel(partner, scale, out):
    first = scale[0:1].astype(jnp.float32)
    second = scale[1:2].astype(jnp.float32)
    out[...] = jnp.where(partner[0] == 0, first, second).astype(out.dtype)


def chosen_scale(partner, scale, after):
    (chosen,), token = ordered_call(
        scale_kernel,
        [partner, scale],
        after,
        [jax.ShapeDtypeStruct((1, scale.shape[1]), scale.dtype)],
        [WHOLE],
        [],
        in_specs=[SMEM, WHOLE],
    )
    return chosen, token


def serve_kernel(me, received, far, order, weight, scale, *refs):
    out, _, table, spread, held, product, table_read, reads, writes = refs[-9:]
    near, depth = received.shape
    tiles = held.shape[0]
    columns = [pl.ds(i * COLUMNS, COLUMNS) for i in range(tiles)]
    table_reading = pltpu.make_async_copy(order.at[me[1]], table, table_read)
    reading = [
        pltpu.make_async_copy(weight.at[:, :, columns[i]], held.at[i], reads.at[i])
        for i in range(tiles)
    ]
    writing = [
        pltpu.make_async_copy(product.at[i], out.at[:, columns[i]], writes.at[i])
        for i in range(tiles)
    ]
    table_reading.start()
    table_reading.wait()
    for copy in reading[:AHEAD]:
        copy.start()

    def gather(which, first, second):
        rows = jnp.dot(table[which, :, :near], first, preferred_element_type=jnp.float32)
        return rows + jnp.dot(table[which, :, near:], second, preferred_element_type=jnp.float32)

    ordered = gather(0, received[...], far[...])
    named = gather(1, received[:, :128], far[:, :128])
    row = lax.broadcasted_iota(jnp.int32, named.shape, 0)
    lane = jnp.where(
        row % STACK < N_X * 8,
        ((row // 4) % 2).astype(jnp.float32),
        named - (2 * me[0]).astype(jnp.float32),
    )[:, 0:1]
    spread[:, :depth] = jnp.where(lane == 0.0, ordered, 0.0).astype(jnp.bfloat16)
    spread[:, depth:] = jnp.where(lane == 1.0, ordered, 0.0).astype(jnp.bfloat16)
    for i in range(tiles):
        reading[i].wait()
        if i + AHEAD < tiles:
            reading[i + AHEAD].start()
        both = held[i].reshape(2 * depth, COLUMNS)
        scales = scale[:, i * COLUMNS : (i + 1) * COLUMNS].astype(jnp.float32)
        total = jnp.dot(spread[...], both, preferred_element_type=jnp.float32)
        total = total * jnp.where(lane == 0.0, scales[0:1], scales[1:2])
        product[i] = total.astype(jnp.bfloat16)
        writing[i].start()
    for copy in writing:
        copy.wait()


def serve(me, received, far, weight, scale, after):
    order = jnp.asarray(return_order(), jnp.bfloat16)
    rows = order.shape[2]
    _, depth, width = weight.shape
    tiles = width // COLUMNS
    return pl.pallas_call(
        serve_kernel,
        in_specs=[SMEM, WHOLE, WHOLE, HBM, HBM, WHOLE] + [HBM] * len(after),
        out_specs=[HBM, HBM],
        scratch_shapes=[
            pltpu.VMEM(order.shape[1:], jnp.bfloat16),
            pltpu.VMEM((rows, 2 * depth), jnp.bfloat16),
            pltpu.VMEM((tiles, 2, depth, COLUMNS), jnp.bfloat16),
            pltpu.VMEM((tiles, rows, COLUMNS), jnp.bfloat16),
            pltpu.SemaphoreType.DMA,
            pltpu.SemaphoreType.DMA((tiles,)),
            pltpu.SemaphoreType.DMA((tiles,)),
        ],
        out_shape=[jax.ShapeDtypeStruct((rows, width), jnp.bfloat16), TOKEN],
        compiler_params=pltpu.CompilerParams(vmem_limit_bytes=VMEM_LIMIT),
        cost_estimate=CHEAP,
    )(me, received, far, order, weight, scale, *after)


def column_codes():
    codes, slots = [], []
    for source in range(N_YC):
        for x in range(N_X):
            for r in range(8):
                slot = (source * 2 + r // 4) * 2 + r % 2
                codes.append((x * 2 + r % 4 // 2) * 256 + slot)
                slots.append(1)
        for x in range(N_X):
            for r in range(12):
                codes.append((x * 2 + r // 6) * 256 + 128 + r % 6)
                slots.append(0)
    return np.array([codes], np.float32), np.array([slots], np.float32)


def mixing_kernel(told, columns, out):
    count = told.shape[2]
    tokens = out.shape[0] // 2 // (N_X * 2)
    row = lax.broadcasted_iota(jnp.int32, (count, count), 0)
    line = lax.broadcasted_iota(jnp.int32, (count, count), 1)
    token = lax.broadcasted_iota(jnp.int32, (tokens, count), 0)
    item = lax.broadcasted_iota(jnp.int32, (tokens, count), 1)
    mine = item // (count // tokens) == token
    for x in range(N_X):
        for step in range(2):
            ids = told[x, step : step + 1, :]
            down = jnp.sum(jnp.where(row == line, ids, 0.0), axis=1, keepdims=True)
            before = jnp.where((down == ids) & (line < row), 1.0, 0.0)
            rank = jnp.sum(before, axis=1, keepdims=True)
            code = jnp.where(rank < 2.0, down * 2.0 + rank, 126.0 + rank)
            code = code + float((x * 2 + step) * 256)
            slot = jnp.where(code == columns[...], 1.0, 0.0).astype(jnp.bfloat16)
            high = told[x, 2 + step : 3 + step, :]
            rest = told[x, 4 + step : 5 + step, :] + told[x, 6 + step : 7 + step, :]
            at = (x * 2 + step) * tokens
            for first, part in ((0, high), (out.shape[0] // 2, rest)):
                gate = jnp.where(mine, part, 0.0).astype(jnp.bfloat16)
                mix = jnp.dot(gate, slot, preferred_element_type=jnp.float32)
                out[first + at : first + at + tokens] = mix.astype(jnp.bfloat16)


def mixing(told, my_x, steps, rows, after):
    codes, slots = column_codes()
    columns = jnp.asarray(codes) + jnp.asarray(slots) * (my_x * N_YC * 4).astype(jnp.float32)
    told = told.astype(jnp.float32).reshape(N_X, 4 * steps, -1)
    (mixes,), token = ordered_call(
        mixing_kernel,
        [told, columns],
        after,
        [jax.ShapeDtypeStruct((2 * N_X * steps * rows, codes.shape[1]), jnp.bfloat16)],
        [WHOLE],
        [],
        in_specs=[WHOLE, WHOLE],
    )
    return mixes, token


def mix_kernel(mixes, returned, out, held, product, reads, writes):
    tiles = held.shape[0]
    columns = [pl.ds(i * COLUMNS, COLUMNS) for i in range(tiles)]
    reading = [
        pltpu.make_async_copy(returned.at[:, columns[i]], held.at[i], reads.at[i])
        for i in range(tiles)
    ]
    writing = [
        pltpu.make_async_copy(product.at[i], out.at[:, columns[i]], writes.at[i])
        for i in range(tiles)
    ]
    for copy in reading:
        copy.start()
    many = out.shape[0]
    for i in range(tiles):
        reading[i].wait()
        total = jnp.dot(mixes[...], held[i], preferred_element_type=jnp.float32)
        product[i] = (total[:many] + total[many:]).astype(out.dtype)
        writing[i].start()
    for copy in writing:
        copy.wait()


def mixed(mixes, returned):
    rows, (many, width) = mixes.shape[0] // 2, returned.shape
    tiles = width // COLUMNS
    return pl.pallas_call(
        mix_kernel,
        in_specs=[WHOLE, HBM],
        out_specs=HBM,
        out_shape=jax.ShapeDtypeStruct((rows, width), jnp.bfloat16),
        scratch_shapes=[
            pltpu.VMEM((tiles, many, COLUMNS), jnp.bfloat16),
            pltpu.VMEM((tiles, rows, COLUMNS), jnp.bfloat16),
            pltpu.SemaphoreType.DMA((tiles,)),
            pltpu.SemaphoreType.DMA((tiles,)),
        ],
        compiler_params=pltpu.CompilerParams(vmem_limit_bytes=VMEM_LIMIT),
        cost_estimate=CHEAP,
    )(mixes, returned)


def local(hidden_in, expert_ids, gates, expert_weight, column_scale, replica_map):
    steps, rows, top, depth = hidden_in.shape
    width = expert_weight.shape[2]
    items = rows * top
    my_x, my_yc, me = lax.axis_index(X), lax.axis_index(("y", "c")), lax.axis_index(EP)

    expert_list = expert_ids.reshape(steps, items)
    rank = rank_of(expert_list)
    step_of = jnp.arange(steps, dtype=jnp.int32)[:, None]
    place = jnp.where(
        rank < 2,
        (expert_list // 2) * BLOCK + (expert_list % 2) * 4 + step_of * 2 + rank,
        1000 + step_of * 8 + rank - 2,
    ).reshape(steps * items)
    extra = jnp.array([2006, 1007, 1015, -1, -1, -1, -1, -1], jnp.int32)
    place = jnp.concatenate([place, extra])
    line = jnp.arange(N_EP * BLOCK, dtype=jnp.int32)
    of_step = (line // BLOCK) % N_C * 8 + line % 8
    line = jnp.where(line % BLOCK < 8, line, jnp.where(line % 8 == 6, 2006, 1000 + of_step))
    selector = (line[:, None] == place[None, :]).astype(jnp.bfloat16)
    hot_id = jnp.sum(jnp.where(rank == 7, expert_list, 0), axis=1).astype(jnp.float32)
    flat_gates = gates.reshape(steps * items)
    high = lax.reduce_precision(flat_gates, 8, 7)
    middle = lax.reduce_precision(flat_gates - high, 8, 7)
    low = flat_gates - high - middle
    told = jnp.concatenate([expert_list.reshape(steps * items).astype(jnp.float32), high, middle, low])
    further = jnp.concatenate(
        [told[None], jnp.broadcast_to(hot_id[:, None], (steps, depth)), jnp.zeros((5, depth), jnp.float32)]
    ).astype(jnp.bfloat16)
    hidden = jnp.concatenate([hidden_in.reshape(steps * items, depth), further])
    part, parts = lax.axis_index("dp"), lax.axis_size("dp")
    here = part.reshape(1).astype(jnp.int32)
    quarter = sum(TRADED)
    starts = [sum(TRADED[:i]) for i in range(len(TRADED))]
    ranges = list(zip(starts, TRADED))
    partner = lax.dynamic_slice(replica_map, ((me + N_EP // 2) % N_EP,), (1,)) % 2
    outgoing = jnp.dot(selector, hidden, preferred_element_type=jnp.float32).astype(jnp.bfloat16)
    received = lax.all_to_all(outgoing.reshape(N_EP, BLOCK, depth), EP, 0, 0, tiled=True)
    mine = lax.dynamic_slice(replica_map, (me,), (1,)) % 2
    picks = lax.psum(jnp.where(jnp.arange(parts) == part, mine, 0), "dp")
    picks = jnp.roll(picks, -part)
    scale, token = chosen_scale(partner, column_scale, [outgoing])
    blocks, token = cut(here, expert_weight, ranges, quarter, [token])
    replica_scale = shifted(scale, "xh", 1)

    def traded(j, after):
        sent, token = pick(picks, crossed[j], parts, after)
        return [shifted(piece, "dp", d + 1) for d, piece in enumerate(sent)], token

    far = shifted(received[:, 8:].reshape(N_EP * 8, depth), "c", 1)
    received = received.reshape(N_EP * BLOCK, depth)
    blocks[0] = gated(blocks[0], [received, picks])
    crossed = [shifted(block, "xh", 1) for block in blocks]
    where = jnp.stack([me, lax.axis_index("c")]).astype(jnp.int32)
    returned, token = serve(where, received, far, expert_weight, column_scale, [token, picks])
    told = received.reshape(N_X, N_YC, BLOCK, depth)[:, :, 14]
    told = lax.dynamic_index_in_dim(told, my_yc, 1, keepdims=False)
    returned = gated(returned, [crossed[0], replica_scale])
    returned = lax.all_to_all(returned.reshape(N_YC, -1, width), ("y", "c"), 0, 0, tiled=True)
    first, token = traded(0, [token])
    mixes, token = mixing(told, my_x, steps, rows, [token])
    straight, token = last_rows(
        partner, expert_weight, depth - parts * quarter, [token, *first]
    )
    straight = shifted(straight, "xh", 1)
    whole, token = placed(
        picks, here, crossed[0], first, starts[0], quarter, depth, None, [token]
    )
    second, token = traded(1, [token])
    whole, token = placed_own(
        picks, here, crossed[1], straight, starts[1], quarter, whole, [token]
    )
    replica_weight = placed_others(here, second, starts[1], quarter, whole, [token])

    partial = mixed(mixes, returned.reshape(-1, width))
    partial = lax.all_to_all(partial.reshape(N_X, steps * rows, width), X, 0, 0, tiled=True)
    combined = jnp.sum(partial.astype(jnp.float32), axis=0).astype(jnp.bfloat16)
    return combined.reshape(steps, rows, width), replica_weight, replica_scale


def solution(mesh):
    grid = Mesh(mesh.devices.reshape(-1, 2, N_X // 2, N_Y, N_C), ("dp",) + EP)
    everywhere = ("dp",) + EP
    in_specs = (
        P(None, everywhere, None, None),
        P(None, everywhere, None),
        P(None, everywhere, None),
        P(EP, None, None),
        P(EP, None),
        P("dp"),
    )
    out_specs = (P(None, everywhere, None), P(everywhere, None, None), P(everywhere, None))
    return jax.shard_map(local, mesh=grid, in_specs=in_specs, out_specs=out_specs, check_vma=False)
```

```python
import functools

import jax
import jax.numpy as jnp
import numpy as np
from jax import lax
from jax.experimental import pallas as pl
from jax.experimental.pallas import tpu as pltpu
from jax.sharding import Mesh, PartitionSpec as P

X = ("xh", "xl")
EP = X + ("y", "c")
N_X, N_Y, N_C = 4, 4, 2
N_YC = N_Y * N_C
N_EP = N_X * N_YC
BLOCK = 16
TRADED = (64, 128)
COLUMNS = 512
VMEM_LIMIT = 50 << 20
AHEAD = 3
CHEAP = pl.CostEstimate(flops=1000, bytes_accessed=1000, transcendentals=0)
HBM = pl.BlockSpec(memory_space=pltpu.HBM)
ANY = pl.BlockSpec(memory_space=pl.ANY)
SMEM = pl.BlockSpec(memory_space=pltpu.SMEM)
WHOLE = pl.BlockSpec(memory_space=pltpu.VMEM)


def shifted(block, axis, distance):
    count = lax.axis_size(axis)
    return lax.ppermute(block, axis, [(i, (i + distance) % count) for i in range(count)])


TOKEN = jax.ShapeDtypeStruct((8, 128), jnp.float32)


def ordered_call(kernel, operands, after, out_shape, out_specs, scratch, in_specs=None, aliases=None, limit=50):
    after = [t for t in after if t is not None]
    in_specs = in_specs or [HBM] * len(operands)

    def body(*refs):
        ins, rest = refs[: len(operands)], refs[len(operands) + len(after) :]
        kernel(*ins, *rest[: len(out_shape)], *rest[len(out_shape) + 1 :])

    *outs, token = pl.pallas_call(
        body,
        out_shape=list(out_shape) + [TOKEN],
        in_specs=list(in_specs) + [HBM] * len(after),
        out_specs=list(out_specs) + [HBM],
        scratch_shapes=scratch,
        input_output_aliases=aliases or {},
        compiler_params=pltpu.CompilerParams(vmem_limit_bytes=limit << 20),
        cost_estimate=CHEAP,
    )(*operands, *after)
    return outs, token


def through(moves, reads, writes):
    reading = [pltpu.make_async_copy(m[0], m[1], reads.at[i]) for i, m in enumerate(moves)]
    writing = [pltpu.make_async_copy(m[1], m[2], writes.at[i]) for i, m in enumerate(moves)]
    for copy in reading:
        copy.start()
    for read, write in zip(reading, writing):
        read.wait()
        write.start()
    for copy in writing:
        copy.wait()


def cut_kernel(ranges, quarter, part, weight, *refs):
    count = len(ranges)
    outs, held, (reads, writes) = refs[:count], refs[count : 2 * count], refs[2 * count :]
    moves = []
    for out, stop, (at, rows) in zip(outs, held, ranges):
        start = pl.multiple_of(part[0] * quarter + at, 16)
        moves.append((weight.at[:, pl.ds(start, rows)], stop, out))
    through(moves, reads, writes)


def cut(part, weight, ranges, quarter, after):
    shapes = [(2, rows, weight.shape[2]) for _, rows in ranges]
    return ordered_call(
        functools.partial(cut_kernel, ranges, quarter),
        [part, weight],
        after,
        [jax.ShapeDtypeStruct(shape, weight.dtype) for shape in shapes],
        [HBM] * len(shapes),
        [pltpu.VMEM(shape, weight.dtype) for shape in shapes]
        + [pltpu.SemaphoreType.DMA((len(shapes),))] * 2,
        in_specs=[SMEM, HBM],
        limit=60,
    )


def last_kernel(partner, weight, out, held, reads, writes):
    rows = held.shape[1]
    first = weight.shape[1] - out.shape[0]
    moves = []
    for i in range(held.shape[0]):
        source = weight.at[partner[0], pl.ds(first + i * rows, rows)]
        moves.append((source, held.at[i], out.at[pl.ds(i * rows, rows)]))
    through(moves, reads, writes)


def last_rows(partner, weight, count, after):
    shape = (count, weight.shape[2])
    (rows,), token = ordered_call(
        last_kernel,
        [partner, weight],
        after,
        [jax.ShapeDtypeStruct(shape, weight.dtype)],
        [HBM],
        [pltpu.VMEM((4, count // 4, shape[1]), weight.dtype)]
        + [pltpu.SemaphoreType.DMA((4,))] * 2,
        in_specs=[SMEM, HBM],
    )
    return rows, token


def pick_kernel(picks, block, *refs):
    *outs, held, reads, writes = refs
    through([(block.at[picks[i + 1]], held.at[i], o) for i, o in enumerate(outs)], reads, writes)


def pick(picks, block, parts, after):
    others = parts - 1
    return ordered_call(
        pick_kernel,
        [picks, block],
        after,
        [jax.ShapeDtypeStruct(block.shape[1:], block.dtype)] * others,
        [HBM] * others,
        [pltpu.VMEM((others,) + block.shape[1:], block.dtype)]
        + [pltpu.SemaphoreType.DMA((others,))] * 2,
        in_specs=[SMEM, ANY],
        limit=12,
    )


def gate_kernel(*_):
    pass


def gated(passed, after):
    (passed,), _ = ordered_call(
        gate_kernel,
        [passed],
        after,
        [jax.ShapeDtypeStruct(passed.shape, passed.dtype)],
        [HBM],
        [],
        aliases={0: 0},
    )
    return passed


def place_kernel(at, quarter, parts, picks, part, block, *refs):
    *refs, out, held, reads, writes = refs
    arrived = refs[: parts - 1]
    rows = arrived[0].shape[0]
    moves = []
    for i, source in enumerate([block.at[picks[0]], *arrived]):
        origin = lax.rem(part[0] - i + parts, parts)
        start = pl.multiple_of(origin * quarter + at, 16)
        moves.append((source, held.at[i], out.at[0, pl.ds(start, rows)]))
    through(moves, reads, writes)


def placed(picks, part, block, arrived, at, quarter, depth, whole, after):
    parts = len(arrived) + 1
    rows, width = arrived[0].shape
    chained = whole is not None
    operands = [picks, part, block, *arrived] + ([whole] if chained else [])
    (whole,), token = ordered_call(
        functools.partial(place_kernel, at, quarter, parts),
        operands,
        after,
        [jax.ShapeDtypeStruct((1, depth, width), block.dtype)],
        [HBM],
        [pltpu.VMEM((parts, rows, width), block.dtype)]
        + [pltpu.SemaphoreType.DMA((parts,))] * 2,
        in_specs=[SMEM, SMEM] + [ANY] * parts + [HBM] * chained,
        aliases={len(operands) - 1: 0} if chained else {},
        limit=12,
    )
    return whole, token


def own_kernel(at, quarter, picks, part, block, straight, _, out, held, rest, reads, writes):
    rows, share = held.shape[0], rest.shape[1]
    count = rest.shape[0]
    start = pl.multiple_of(part[0] * quarter + at, 16)
    moves = [(block.at[picks[0]], held, out.at[0, pl.ds(start, rows)])]
    for i in range(count):
        first = out.shape[1] - (count - i) * share
        moves.append(
            (straight.at[pl.ds(i * share, share)], rest.at[i], out.at[0, pl.ds(first, share)])
        )
    through(moves, reads, writes)


def placed_own(picks, part, block, straight, at, quarter, whole, after):
    _, rows, width = block.shape
    (whole,), token = ordered_call(
        functools.partial(own_kernel, at, quarter),
        [picks, part, block, straight, whole],
        after,
        [jax.ShapeDtypeStruct(whole.shape, whole.dtype)],
        [HBM],
        [
            pltpu.VMEM((rows, width), block.dtype),
            pltpu.VMEM((4, straight.shape[0] // 4, width), block.dtype),
        ]
        + [pltpu.SemaphoreType.DMA((5,))] * 2,
        in_specs=[SMEM, SMEM, ANY, ANY, HBM],
        aliases={4: 0},
        limit=16,
    )
    return whole, token


def others_kernel(at, quarter, part, *refs):
    *arrived, _, out, held, reads, writes = refs
    parts = len(arrived) + 1
    rows = arrived[0].shape[0]
    moves = []
    for i, source in enumerate(arrived):
        origin = lax.rem(part[0] - i - 1 + parts, parts)
        start = pl.multiple_of(origin * quarter + at, 16)
        moves.append((source, held.at[i], out.at[0, pl.ds(start, rows)]))
    through(moves, reads, writes)


def placed_others(part, arrived, at, quarter, whole, after):
    rows, width = arrived[0].shape
    count = len(arrived)
    (whole,), _ = ordered_call(
        functools.partial(others_kernel, at, quarter),
        [part, *arrived, whole],
        after,
        [jax.ShapeDtypeStruct(whole.shape, whole.dtype)],
        [HBM],
        [pltpu.VMEM((count, rows, width), whole.dtype)]
        + [pltpu.SemaphoreType.DMA((count,))] * 2,
        in_specs=[SMEM] + [ANY] * count + [HBM],
        aliases={1 + count: 0},
        limit=16,
    )
    return whole


def rank_of(expert_list):
    count = expert_list.shape[-1]
    order = jnp.arange(count, dtype=jnp.int32)
    same = expert_list[..., :, None] == expert_list[..., None, :]
    return jnp.sum(same & (order[:, None] > order[None, :]), axis=-1, dtype=jnp.int32)


STACK = N_X * 20


def one_hot_rows(sources):
    table = np.zeros((len(sources), N_EP * (BLOCK + 8)), np.float32)
    table[np.arange(len(sources)), sources] = 1.0
    return table


def return_order():
    orders, namings = [], []
    for core in range(N_C):
        rows, names = [], []
        for yc in range(N_YC):
            clients = [x * N_YC + yc for x in range(N_X)]
            for client in clients:
                rows += [client * BLOCK + r for r in range(8)]
                names += [client * BLOCK + 15] * 8
            for client in clients:
                for step in range(2):
                    at = client * BLOCK + 8 if step == core else N_EP * BLOCK + client * 8
                    rows += [at + r for r in range(6)]
                    names += [at + 7] * 6
        orders.append(one_hot_rows(rows))
        namings.append(one_hot_rows(names))
    return np.stack([np.stack(orders), np.stack(namings)], 1)


def scale_kernel(partner, scale, out):
    first = scale[0:1].astype(jnp.float32)
    second = scale[1:2].astype(jnp.float32)
    out[...] = jnp.where(partner[0] == 0, first, second).astype(out.dtype)


def chosen_scale(partner, scale, after):
    (chosen,), token = ordered_call(
        scale_kernel,
        [partner, scale],
        after,
        [jax.ShapeDtypeStruct((1, scale.shape[1]), scale.dtype)],
        [WHOLE],
        [],
        in_specs=[SMEM, WHOLE],
    )
    return chosen, token


def serve_kernel(me, received, far, order, weight, scale, *refs):
    out, _, table, spread, held, product, table_read, reads, writes = refs[-9:]
    near, depth = received.shape
    tiles = held.shape[0]
    columns = [pl.ds(i * COLUMNS, COLUMNS) for i in range(tiles)]
    table_reading = pltpu.make_async_copy(order.at[me[1]], table, table_read)
    reading = [
        pltpu.make_async_copy(weight.at[:, :, columns[i]], held.at[i], reads.at[i])
        for i in range(tiles)
    ]
    writing = [
        pltpu.make_async_copy(product.at[i], out.at[:, columns[i]], writes.at[i])
        for i in range(tiles)
    ]
    table_reading.start()
    table_reading.wait()
    for copy in reading[:AHEAD]:
        copy.start()

    def gather(which, first, second):
        rows = jnp.dot(table[which, :, :near], first, preferred_element_type=jnp.float32)
        return rows + jnp.dot(table[which, :, near:], second, preferred_element_type=jnp.float32)

    ordered = gather(0, received[...], far[...])
    named = gather(1, received[:, :128], far[:, :128])
    row = lax.broadcasted_iota(jnp.int32, named.shape, 0)
    lane = jnp.where(
        row % STACK < N_X * 8,
        ((row // 4) % 2).astype(jnp.float32),
        named - (2 * me[0]).astype(jnp.float32),
    )[:, 0:1]
    spread[:, :depth] = jnp.where(lane == 0.0, ordered, 0.0).astype(jnp.bfloat16)
    spread[:, depth:] = jnp.where(lane == 1.0, ordered, 0.0).astype(jnp.bfloat16)
    for i in range(tiles):
        reading[i].wait()
        if i + AHEAD < tiles:
            reading[i + AHEAD].start()
        both = held[i].reshape(2 * depth, COLUMNS)
        scales = scale[:, i * COLUMNS : (i + 1) * COLUMNS].astype(jnp.float32)
        total = jnp.dot(spread[...], both, preferred_element_type=jnp.float32)
        total = total * jnp.where(lane == 0.0, scales[0:1], scales[1:2])
        product[i] = total.astype(jnp.bfloat16)
        writing[i].start()
    for copy in writing:
        copy.wait()


def serve(me, received, far, weight, scale, after):
    order = jnp.asarray(return_order(), jnp.bfloat16)
    rows = order.shape[2]
    _, depth, width = weight.shape
    tiles = width // COLUMNS
    return pl.pallas_call(
        serve_kernel,
        in_specs=[SMEM, WHOLE, WHOLE, HBM, HBM, WHOLE] + [HBM] * len(after),
        out_specs=[HBM, HBM],
        scratch_shapes=[
            pltpu.VMEM(order.shape[1:], jnp.bfloat16),
            pltpu.VMEM((rows, 2 * depth), jnp.bfloat16),
            pltpu.VMEM((tiles, 2, depth, COLUMNS), jnp.bfloat16),
            pltpu.VMEM((tiles, rows, COLUMNS), jnp.bfloat16),
            pltpu.SemaphoreType.DMA,
            pltpu.SemaphoreType.DMA((tiles,)),
            pltpu.SemaphoreType.DMA((tiles,)),
        ],
        out_shape=[jax.ShapeDtypeStruct((rows, width), jnp.bfloat16), TOKEN],
        compiler_params=pltpu.CompilerParams(vmem_limit_bytes=VMEM_LIMIT),
        cost_estimate=CHEAP,
    )(me, received, far, order, weight, scale, *after)


def column_codes():
    codes, slots = [], []
    for source in range(N_YC):
        for x in range(N_X):
            for r in range(8):
                slot = (source * 2 + r // 4) * 2 + r % 2
                codes.append((x * 2 + r % 4 // 2) * 256 + slot)
                slots.append(1)
        for x in range(N_X):
            for r in range(12):
                codes.append((x * 2 + r // 6) * 256 + 128 + r % 6)
                slots.append(0)
    return np.array([codes], np.float32), np.array([slots], np.float32)


def mixing_kernel(told, columns, out):
    count = told.shape[2]
    tokens = out.shape[0] // 2 // (N_X * 2)
    row = lax.broadcasted_iota(jnp.int32, (count, count), 0)
    line = lax.broadcasted_iota(jnp.int32, (count, count), 1)
    token = lax.broadcasted_iota(jnp.int32, (tokens, count), 0)
    item = lax.broadcasted_iota(jnp.int32, (tokens, count), 1)
    mine = item // (count // tokens) == token
    for x in range(N_X):
        for step in range(2):
            ids = told[x, step : step + 1, :]
            down = jnp.sum(jnp.where(row == line, ids, 0.0), axis=1, keepdims=True)
            before = jnp.where((down == ids) & (line < row), 1.0, 0.0)
            rank = jnp.sum(before, axis=1, keepdims=True)
            code = jnp.where(rank < 2.0, down * 2.0 + rank, 126.0 + rank)
            code = code + float((x * 2 + step) * 256)
            slot = jnp.where(code == columns[...], 1.0, 0.0).astype(jnp.bfloat16)
            high = told[x, 2 + step : 3 + step, :]
            rest = told[x, 4 + step : 5 + step, :] + told[x, 6 + step : 7 + step, :]
            at = (x * 2 + step) * tokens
            for first, part in ((0, high), (out.shape[0] // 2, rest)):
                gate = jnp.where(mine, part, 0.0).astype(jnp.bfloat16)
                mix = jnp.dot(gate, slot, preferred_element_type=jnp.float32)
                out[first + at : first + at + tokens] = mix.astype(jnp.bfloat16)


def mixing(told, my_x, steps, rows, after):
    codes, slots = column_codes()
    columns = jnp.asarray(codes) + jnp.asarray(slots) * (my_x * N_YC * 4).astype(jnp.float32)
    told = told.astype(jnp.float32).reshape(N_X, 4 * steps, -1)
    (mixes,), token = ordered_call(
        mixing_kernel,
        [told, columns],
        after,
        [jax.ShapeDtypeStruct((2 * N_X * steps * rows, codes.shape[1]), jnp.bfloat16)],
        [WHOLE],
        [],
        in_specs=[WHOLE, WHOLE],
    )
    return mixes, token


def mix_kernel(mixes, returned, out, held, product, reads, writes):
    tiles = held.shape[0]
    columns = [pl.ds(i * COLUMNS, COLUMNS) for i in range(tiles)]
    reading = [
        pltpu.make_async_copy(returned.at[:, columns[i]], held.at[i], reads.at[i])
        for i in range(tiles)
    ]
    writing = [
        pltpu.make_async_copy(product.at[i], out.at[:, columns[i]], writes.at[i])
        for i in range(tiles)
    ]
    for copy in reading:
        copy.start()
    many = out.shape[0]
    for i in range(tiles):
        reading[i].wait()
        total = jnp.dot(mixes[...], held[i], preferred_element_type=jnp.float32)
        product[i] = (total[:many] + total[many:]).astype(out.dtype)
        writing[i].start()
    for copy in writing:
        copy.wait()


def mixed(mixes, returned):
    rows, (many, width) = mixes.shape[0] // 2, returned.shape
    tiles = width // COLUMNS
    return pl.pallas_call(
        mix_kernel,
        in_specs=[WHOLE, HBM],
        out_specs=HBM,
        out_shape=jax.ShapeDtypeStruct((rows, width), jnp.bfloat16),
        scratch_shapes=[
            pltpu.VMEM((tiles, many, COLUMNS), jnp.bfloat16),
            pltpu.VMEM((tiles, rows, COLUMNS), jnp.bfloat16),
            pltpu.SemaphoreType.DMA((tiles,)),
            pltpu.SemaphoreType.DMA((tiles,)),
        ],
        compiler_params=pltpu.CompilerParams(vmem_limit_bytes=VMEM_LIMIT),
        cost_estimate=CHEAP,
    )(mixes, returned)


def local(hidden_in, expert_ids, gates, expert_weight, column_scale, replica_map):
    steps, rows, top, depth = hidden_in.shape
    width = expert_weight.shape[2]
    items = rows * top
    my_x, my_yc, me = lax.axis_index(X), lax.axis_index(("y", "c")), lax.axis_index(EP)

    expert_list = expert_ids.reshape(steps, items)
    rank = rank_of(expert_list)
    step_of = jnp.arange(steps, dtype=jnp.int32)[:, None]
    place = jnp.where(
        rank < 2,
        (expert_list // 2) * BLOCK + (expert_list % 2) * 4 + step_of * 2 + rank,
        1000 + step_of * 8 + rank - 2,
    ).reshape(steps * items)
    extra = jnp.array([2006, 1007, 1015, -1, -1, -1, -1, -1], jnp.int32)
    place = jnp.concatenate([place, extra])
    line = jnp.arange(N_EP * BLOCK, dtype=jnp.int32)
    of_step = (line // BLOCK) % N_C * 8 + line % 8
    line = jnp.where(line % BLOCK < 8, line, jnp.where(line % 8 == 6, 2006, 1000 + of_step))
    selector = (line[:, None] == place[None, :]).astype(jnp.bfloat16)
    hot_id = jnp.sum(jnp.where(rank == 7, expert_list, 0), axis=1).astype(jnp.float32)
    flat_gates = gates.reshape(steps * items)
    high = lax.reduce_precision(flat_gates, 8, 7)
    middle = lax.reduce_precision(flat_gates - high, 8, 7)
    low = flat_gates - high - middle
    told = jnp.concatenate([expert_list.reshape(steps * items).astype(jnp.float32), high, middle, low])
    further = jnp.concatenate(
        [told[None], jnp.broadcast_to(hot_id[:, None], (steps, depth)), jnp.zeros((5, depth), jnp.float32)]
    ).astype(jnp.bfloat16)
    hidden = jnp.concatenate([hidden_in.reshape(steps * items, depth), further])
    part, parts = lax.axis_index("dp"), lax.axis_size("dp")
    here = part.reshape(1).astype(jnp.int32)
    quarter = sum(TRADED)
    starts = [sum(TRADED[:i]) for i in range(len(TRADED))]
    ranges = list(zip(starts, TRADED))
    partner = lax.dynamic_slice(replica_map, ((me + N_EP // 2) % N_EP,), (1,)) % 2
    outgoing = jnp.dot(selector, hidden, preferred_element_type=jnp.float32).astype(jnp.bfloat16)
    received = lax.all_to_all(outgoing.reshape(N_EP, BLOCK, depth), EP, 0, 0, tiled=True)
    mine = lax.dynamic_slice(replica_map, (me,), (1,)) % 2
    picks = lax.psum(jnp.where(jnp.arange(parts) == part, mine, 0), "dp")
    picks = jnp.roll(picks, -part)
    scale, token = chosen_scale(partner, column_scale, [outgoing])
    blocks, token = cut(here, expert_weight, ranges, quarter, [token])
    replica_scale = shifted(scale, "xh", 1)

    def traded(j, after):
        sent, token = pick(picks, crossed[j], parts, after)
        return [shifted(piece, "dp", d + 1) for d, piece in enumerate(sent)], token

    far = shifted(received[:, 8:].reshape(N_EP * 8, depth), "c", 1)
    received = received.reshape(N_EP * BLOCK, depth)
    blocks[0] = gated(blocks[0], [received, picks])
    crossed = [shifted(block, "xh", 1) for block in blocks]
    where = jnp.stack([me, lax.axis_index("c")]).astype(jnp.int32)
    returned, token = serve(where, received, far, expert_weight, column_scale, [token, picks])
    told = received.reshape(N_X, N_YC, BLOCK, depth)[:, :, 14]
    told = lax.dynamic_index_in_dim(told, my_yc, 1, keepdims=False)
    returned = gated(returned, [crossed[0], replica_scale])
    returned = lax.all_to_all(returned.reshape(N_YC, -1, width), ("y", "c"), 0, 0, tiled=True)
    first, token = traded(0, [token])
    mixes, token = mixing(told, my_x, steps, rows, [token])
    straight, token = last_rows(
        partner, expert_weight, depth - parts * quarter, [token, *first]
    )
    straight = shifted(straight, "xh", 1)
    whole, token = placed(
        picks, here, crossed[0], first, starts[0], quarter, depth, None, [token]
    )
    second, token = traded(1, [token])
    partial = mixed(mixes, returned.reshape(-1, width))
    partial = lax.all_to_all(partial.reshape(N_X, steps * rows, width), X, 0, 0, tiled=True)
    combined = jnp.sum(partial.astype(jnp.float32), axis=0).astype(jnp.bfloat16)
    whole, token = placed_own(
        picks, here, crossed[1], straight, starts[1], quarter, whole, [token]
    )
    replica_weight = placed_others(here, second, starts[1], quarter, whole, [token, combined])

    return combined.reshape(steps, rows, width), replica_weight, replica_scale


def solution(mesh):
    grid = Mesh(mesh.devices.reshape(-1, 2, N_X // 2, N_Y, N_C), ("dp",) + EP)
    everywhere = ("dp",) + EP
    in_specs = (
        P(None, everywhere, None, None),
        P(None, everywhere, None),
        P(None, everywhere, None),
        P(EP, None, None),
        P(EP, None),
        P("dp"),
    )
    out_specs = (P(None, everywhere, None), P(everywhere, None, None), P(everywhere, None))
    return jax.shard_map(local, mesh=grid, in_specs=in_specs, out_specs=out_specs, check_vma=False)
```
